128 devices in a mesh: tm: 2 (over x_lo), rows: 64 (over z, y, x_hi, core), roll: 1.
Axes of the slice: x: 4 (x_hi: 2, x_lo: 2; x = x_hi * 2 + x_lo), y: 4, z: 4, core: 2. Of those that a mesh axis runs over, the one named last changes fastest.
Arguments:
- frames_in: bfloat16 [8, 256, 160, 192], P('tm', 'rows', 'roll'), may hold values from -6 to 6
- gain_one: float32 [192], replicated, may hold values from 0.25 to 1.75
- conv_one: bfloat16 [3, 3, 3, 192, 192], replicated, may hold values from -0.078125 to 0.078125
- bias_one: float32 [192], replicated, may hold values from -3 to 3
- gain_two: float32 [192], replicated, may hold values from 0.25 to 1.75
- conv_two: bfloat16 [3, 3, 3, 192, 192], replicated, may hold values from -0.078125 to 0.078125
- bias_two: float32 [192], replicated, may hold values from -3 to 3
Outputs:
- frames_out: bfloat16 [8, 256, 160, 192], P('tm', 'rows', 'roll')
The draws below stay inside these ranges and needn't reach their ends.
All inputs are finite; a program needn't handle non-finite values.
Results may differ from the reference program's by a relative error of at most 0.0034.
Values may be sent and summed in bfloat16 or wider, within the bound.
No kernel may reach another device: no remote copies, remote signals or barrier semaphores. Data moves between devices by JAX's collectives and lax.ppermute only.
A program may use at most 256 MiB of HBM per device.

```python
import jax
import jax.numpy as jnp
from jax import lax

C = 192
W = 160
FRAMES = 8
ROWS = 256


def steps_of(rng, extent, shards, low, top_value):
    level, own = 1.0, jax.random.fold_in(rng, 6)
    for axis_at, parts in shards:
        heights = jnp.exp(jax.random.uniform(jax.random.fold_in(own, axis_at), (parts,), jnp.float32, low / len(shards), top_value / len(shards)))
        level = level * jnp.repeat(heights, extent[axis_at] // parts).reshape([-1 if axis == axis_at else 1 for axis in range(len(extent))])
    return level


def gaussian(own_key, shape, deviation, bound, split=(), held_as=jnp.bfloat16):
    result = deviation * jax.random.normal(own_key, shape, jnp.float32)
    if split:
        result = result * steps_of(own_key, shape, split, -0.22, 0.18)
    return jnp.clip(result, -bound, bound).astype(held_as)


def setup_inputs(seed: int = 0, part: int = 0) -> dict:
    seeds = jax.random.split(jax.random.key(seed), 8)
    own_keys = jax.random.split(jax.random.fold_in(seeds[7], part), 8)
    return {
        "frames_in": gaussian(own_keys[0], (FRAMES, ROWS, W, C), 1.0, 6.0, ((0, 2), (1, 64))),
        "gain_one": jnp.clip(1.0 + 0.15 * jax.random.normal(seeds[1], (C,), jnp.float32), 0.25, 1.75),
        "conv_one": gaussian(seeds[2], (3, 3, 3, C, C), (27 * C) ** -0.5, 0.078125),
        "bias_one": gaussian(seeds[3], (C,), 0.5, 3.0, (), jnp.float32),
        "gain_two": jnp.clip(1.0 + 0.15 * jax.random.normal(seeds[4], (C,), jnp.float32), 0.25, 1.75),
        "conv_two": gaussian(seeds[5], (3, 3, 3, C, C), (27 * C) ** -0.5, 0.078125),
        "bias_two": gaussian(seeds[6], (C,), 0.5, 3.0, (), jnp.float32),
    }


def normalize(values, gain):
    power = lax.optimization_barrier(jnp.mean(values * values, axis=-1, keepdims=True))
    return jax.nn.silu(values * jax.lax.rsqrt(power + 1e-06) * gain)

def convolve(extended, weight, offset):
    frames_out = extended.shape[0] - 2
    rows_out = extended.shape[1] - 2
    across = extended.shape[2]
    chans = extended.shape[3]
    padded = jnp.pad(extended, ((0, 0), (0, 0), (1, 1), (0, 0)))
    columns = jnp.concatenate([padded[:, shift_row:shift_row + rows_out, shift_col:shift_col + across, :] for shift_row in range(3) for shift_col in range(3)], axis=-1)
    tap_table = weight.reshape(3, 9 * chans, weight.shape[-1])
    summed = jnp.zeros((frames_out * rows_out * across, weight.shape[-1]), jnp.float32) + offset.astype(jnp.float32)
    for step_time in range(3):
        slab_part = columns[step_time:step_time + frames_out].reshape(-1, 9 * chans)
        summed = summed + jnp.dot(slab_part, tap_table[step_time], preferred_element_type=jnp.float32)
    return summed.reshape(frames_out, rows_out, across, weight.shape[-1])

def reference(frames_in, gain_one, conv_one, bias_one, gain_two, conv_two, bias_two):
    start = frames_in.astype(jnp.float32)
    first = normalize(start, gain_one).astype(jnp.bfloat16)
    inner = convolve(jnp.pad(first, ((2, 0), (1, 1), (0, 0), (0, 0))), conv_one, bias_one)
    second = normalize(inner, gain_two).astype(jnp.bfloat16)
    outer = convolve(jnp.pad(second, ((2, 0), (1, 1), (0, 0), (0, 0))), conv_two, bias_two)
    return (start + outer).astype(jnp.bfloat16)
```

```python
import functools

import jax
import jax.numpy as jnp
import numpy as np
from jax import lax
from jax.experimental import pallas as pl
from jax.experimental.pallas import tpu as pltpu
from jax.sharding import PartitionSpec as P

BF = jnp.bfloat16
F32 = jnp.float32
C = 192
W = 160
S = 16
J = W // S
E = W + 2 * S
MB = 2**20


def spread():
    m = np.zeros((E, W), np.float32)
    for jj in range(J + 2):
        for s in range(S):
            c = s * J + jj - 1
            if 0 <= c < W:
                m[jj * S + s, c] = 1
    return m


def gather():
    return spread()[S : S + W].T.copy()


def flip(n, par):
    return n + par * (3 - 2 * n)


def act(v, gain):
    power = jnp.mean(v * v, axis=-1, keepdims=True)
    h = v * lax.rsqrt(power + 1e-06) * (gain * 0.5)
    return h + h * jnp.tanh(h)


def pack(v):
    hi = v[:, 128:]
    return jnp.concatenate([v[:, :128], jnp.concatenate([hi[:80], hi[80:]], axis=1)], axis=0)


def unpack(d):
    hi = d[W:]
    return jnp.concatenate([d[:W], jnp.concatenate([hi[:, :64], hi[:, 64:]], axis=0)], axis=1)


def put(ref, at, v):
    ref[at + (slice(S, S + W), slice(0, C))] = v
    spot = lax.broadcasted_iota(jnp.int32, (S, C), 0)
    last = pltpu.roll(v[W - S :].astype(F32), 1, 0)
    head = pltpu.roll(v[:S].astype(F32), S - 1, 0)
    ref[at + (slice(0, S), slice(0, C))] = jnp.where(spot == 0, 0.0, last).astype(BF)
    ref[at + (slice(S + W, E), slice(0, C))] = jnp.where(spot == S - 1, 0.0, head).astype(BF)


def taps(acc, src, tau, v, w, par, offs):
    for a in offs:
        for p in range(3):
            for q in range(3):
                wt = w[a, p + par * (2 - 2 * p), q]
                blk = src[tau + a, v + p, S * q : S * q + W, :]
                acc = acc + jnp.dot(blk, wt, preferred_element_type=F32)
    return acc


def prep_kernel(x_ref, g_ref, m_ref, own_ref, b_ref, a_ref, t_ref, d_ref):
    par = lax.axis_index("rows") % 2
    t = pl.program_id(0)
    g = g_ref[...]
    for u in range(4):
        xr = x_ref[0, flip(u, par)]
        xp = jnp.dot(m_ref[...], xr, preferred_element_type=F32)
        f = act(xp, g).astype(BF)
        own_ref[0, u] = f
        d = pack(f[S : S + W])
        if u < 2:
            b_ref[0, u] = d
            d_ref[0, u] = d
        else:
            a_ref[0, 3 - u] = d
        t_ref[0, u] = d


def mid_kernel(own_ref, b_ref, a_ref, w1_ref, w2_ref, bias_ref, g_ref, s_ref, p_ref, x_ref):
    r = lax.axis_index("rows")
    par = r % 2
    for t in range(4):
        for u in range(4):
            x_ref[t, u + 2] = own_ref[t, u]
        for k in range(2):
            put(x_ref, (t, 1 - k), unpack(b_ref[t, k]))
            put(x_ref, (t, 6 + k), unpack(a_ref[t, k]))
    inside = jnp.where((r == 0) | (r == 63), 0.0, 1.0).astype(F32)
    bias = bias_ref[...]
    g = g_ref[...]

    def row(v, _):
        keep = jnp.where(v == 0, inside, 1.0)
        for tau in range(2):
            acc = taps(jnp.zeros((W, C), F32), x_ref, tau, v, w1_ref, par, range(3))
            put(s_ref, (tau, v), (act(acc + bias, g) * keep).astype(BF))
        return 0

    lax.fori_loop(0, 6, row, 0)

    def part(u, _):
        acc0 = taps(jnp.zeros((W, C), F32), s_ref, 0, u, w2_ref, par, (0, 1))
        p_ref[0, u] = pack(acc0.astype(BF))
        acc1 = taps(jnp.zeros((W, C), F32), s_ref, 1, u, w2_ref, par, (0,))
        p_ref[1, u] = pack(acc1.astype(BF))
        return 0

    lax.fori_loop(0, 4, part, 0)


def late_kernel(
    own_ref, b_ref, a_ref, t_ref, d_ref, c_ref, s23_ref, w1_ref, w2_ref, b1_ref, g_ref, b2_ref,
    in_ref, m_ref, back_ref, out_ref, acc_ref, x_ref, s_ref,
):
    r = lax.axis_index("rows")
    par = r % 2
    for t in range(2):
        for u in range(4):
            x_ref[t + 2, u + 2] = own_ref[t, u]
            put(x_ref, (t, u + 2), unpack(t_ref[t, u]))
        for k in range(2):
            put(x_ref, (t + 2, 1 - k), unpack(b_ref[t, k]))
            put(x_ref, (t + 2, 6 + k), unpack(a_ref[t, k]))
            put(x_ref, (t, 1 - k), unpack(d_ref[t, k]))
            put(x_ref, (t, 6 + k), unpack(c_ref[t, k]))
        for v in range(6):
            s_ref[t + 2, v] = s23_ref[t, v]
    inside = jnp.where((r == 0) | (r == 63), 0.0, 1.0).astype(F32)
    bias = b1_ref[...]
    g = g_ref[...]

    def row(v, _):
        keep = jnp.where(v == 0, inside, 1.0)
        for tau in range(2):
            acc = taps(jnp.zeros((W, C), F32), x_ref, tau, v, w1_ref, par, range(3))
            put(s_ref, (tau, v), (act(acc + bias, g) * keep).astype(BF))
        return 0

    lax.fori_loop(0, 6, row, 0)
    bias2 = b2_ref[...]

    def last(u, _):
        at = flip(u, par)
        for tau in range(4):
            start = jnp.dot(m_ref[S : S + W, :], in_ref[tau, at], preferred_element_type=F32)
            offs = [a for a in range(3) if tau + a >= 2]
            acc = taps(start + bias2, s_ref, tau - 2, u, w2_ref, par, offs)
            if tau < 2:
                acc_ref[tau, u] = acc
            else:
                y = jnp.dot(back_ref[...], acc.astype(BF), preferred_element_type=F32)
                out_ref[tau, at] = y.astype(BF)
        return 0

    lax.fori_loop(0, 4, last, 0)


def add_kernel(acc_ref, p_ref, back_ref, full_ref, out_ref):
    par = lax.axis_index("rows") % 2
    for u in range(4):
        y = (acc_ref[0, u] + unpack(p_ref[0, u]).astype(F32)).astype(BF)
        z = jnp.dot(back_ref[...], y, preferred_element_type=F32)
        out_ref[0, flip(u, par)] = z.astype(BF)


def swap_routes(n):
    near = [(i, i ^ 1) for i in range(n)]
    far = [(i, i + 1) for i in range(1, n - 1, 2)] + [(i + 1, i) for i in range(1, n - 1, 2)]
    return near, far


VMEM = pl.BlockSpec(memory_space=pltpu.VMEM)


def local(frames_in, gain_one, conv_one, bias_one, gain_two, conv_two, bias_two):
    n = lax.axis_size("rows")
    near, far = swap_routes(n)
    diag = [(i, n + j) for i, j in far]
    m = jnp.asarray(spread(), BF)
    back = jnp.asarray(gather(), BF)
    g1, g2 = gain_one.reshape(1, C), gain_two.reshape(1, C)
    b1, b2 = bias_one.reshape(1, C), bias_two.reshape(1, C)
    sds = jax.ShapeDtypeStruct

    own, bs, as_, ts, ds = pl.pallas_call(
        prep_kernel,
        grid=(4,),
        in_specs=[
            pl.BlockSpec((1, 4, W, C), lambda t: (t, 0, 0, 0)),
            pl.BlockSpec((1, C), lambda t: (0, 0)),
            pl.BlockSpec((E, W), lambda t: (0, 0)),
        ],
        out_specs=[
            pl.BlockSpec((1, 4, E, C), lambda t: (t, 0, 0, 0)),
            pl.BlockSpec((1, 2, 240, 128), lambda t: (t, 0, 0, 0)),
            pl.BlockSpec((1, 2, 240, 128), lambda t: (t, 0, 0, 0)),
            pl.BlockSpec((1, 4, 240, 128), lambda t: (jnp.maximum(t - 2, 0), 0, 0, 0)),
            pl.BlockSpec((1, 2, 240, 128), lambda t: (jnp.maximum(t - 2, 0), 0, 0, 0)),
        ],
        out_shape=[
            sds((4, 4, E, C), BF),
            sds((4, 2, 240, 128), BF),
            sds((4, 2, 240, 128), BF),
            sds((2, 4, 240, 128), BF),
            sds((2, 2, 240, 128), BF),
        ],
        compiler_params=pltpu.CompilerParams(vmem_limit_bytes=24 * MB),
        cost_estimate=pl.CostEstimate(flops=300_000_000, bytes_accessed=5_000_000, transcendentals=500_000),
        name="prep",
    )(frames_in, g1, m)

    br = lax.ppermute(bs, "rows", far)
    ar = lax.ppermute(as_, "rows", near)
    tr = lax.ppermute(ts, "tm", [(0, 1)])
    dr = lax.ppermute(ds, ("tm", "rows"), diag)

    s23, ps = pl.pallas_call(
        mid_kernel,
        in_specs=[VMEM] * 7,
        out_specs=[VMEM] * 2,
        out_shape=[sds((2, 6, E, C), BF), sds((2, 4, 240, 128), BF)],
        scratch_shapes=[pltpu.VMEM((4, 8, E, C), BF)],
        compiler_params=pltpu.CompilerParams(vmem_limit_bytes=40 * MB),
        cost_estimate=pl.CostEstimate(flops=10_000_000_000, bytes_accessed=12_000_000, transcendentals=500_000),
        name="mid",
    )(own, br, ar, conv_one, conv_two, b1, g2)

    pr = lax.ppermute(ps, "tm", [(0, 1)])
    cr = lax.ppermute(jnp.stack([tr[:, 3], tr[:, 2]], axis=1), "rows", near)

    out, acc = pl.pallas_call(
        late_kernel,
        in_specs=[VMEM] * 15,
        out_specs=[VMEM] * 2,
        out_shape=[sds((4, 4, W, C), BF), sds((2, 4, W, C), F32)],
        scratch_shapes=[pltpu.VMEM((4, 8, E, C), BF), pltpu.VMEM((4, 6, E, C), BF)],
        compiler_params=pltpu.CompilerParams(vmem_limit_bytes=48 * MB),
        cost_estimate=pl.CostEstimate(flops=16_000_000_000, bytes_accessed=16_000_000, transcendentals=500_000),
        name="late",
    )(own, br, ar, tr, dr, cr, s23, conv_one, conv_two, b1, g2, b2, frames_in, m, back)

    return pl.pallas_call(
        add_kernel,
        grid=(2,),
        in_specs=[
            pl.BlockSpec((1, 4, W, C), lambda t: (t, 0, 0, 0)),
            pl.BlockSpec((1, 4, 240, 128), lambda t: (t, 0, 0, 0)),
            pl.BlockSpec((W, W), lambda t: (0, 0)),
            pl.BlockSpec(memory_space=pl.ANY),
        ],
        out_specs=pl.BlockSpec((1, 4, W, C), lambda t: (t, 0, 0, 0)),
        out_shape=sds((4, 4, W, C), BF),
        input_output_aliases={3: 0},
        compiler_params=pltpu.CompilerParams(vmem_limit_bytes=24 * MB),
        cost_estimate=pl.CostEstimate(flops=100_000_000, bytes_accessed=3_000_000, transcendentals=0),
        name="add",
    )(acc, pr, back, out)


def solution(mesh):
    in_specs = (P("tm", "rows", "roll", None), P(), P(), P(), P(), P(), P())
    out_specs = P("tm", "rows", "roll", None)
    return jax.shard_map(local, mesh=mesh, in_specs=in_specs, out_specs=out_specs, check_vma=False)
```

```python
import jax
import jax.numpy as jnp
from jax import lax
from jax.experimental import pallas as pl
from jax.experimental.pallas import tpu as pltpu
from jax.sharding import PartitionSpec as P

BF = jnp.bfloat16
F32 = jnp.float32
C = 192
W = 160
S = 16
J = W // S
E = W + 2 * S
D = 240
MB = 2**20


def spread(rows, shift):
    n = lax.broadcasted_iota(jnp.int32, (rows, W), 0)
    c = lax.broadcasted_iota(jnp.int32, (rows, W), 1)
    return jnp.where((n & (S - 1)) * J + (n >> 4) - shift == c, 1.0, 0.0).astype(BF)


def gather():
    c = lax.broadcasted_iota(jnp.int32, (W, W), 0)
    n = lax.broadcasted_iota(jnp.int32, (W, W), 1)
    return jnp.where((n & (S - 1)) * J + (n >> 4) == c, 1.0, 0.0).astype(BF)


def flip(n, par):
    return n + par * (3 - 2 * n)


def act(v, gain):
    power = jnp.mean(v * v, axis=-1, keepdims=True)
    h = v * lax.rsqrt(power + 1e-06) * (gain * 0.5)
    return h + h * jnp.tanh(h)


def pack(v):
    hi = v[:, 128:]
    return jnp.concatenate([v[:, :128], jnp.concatenate([hi[:80], hi[80:]], axis=1)], axis=0)


def unpack(d):
    hi = d[W:]
    return jnp.concatenate([d[:W], jnp.concatenate([hi[:, :64], hi[:, 64:]], axis=0)], axis=1)


def put(ref, at, v):
    ref[at + (slice(S, S + W), slice(0, C))] = v
    spot = lax.broadcasted_iota(jnp.int32, (S, C), 0)
    last = pltpu.roll(v[W - S :].astype(F32), 1, 0)
    head = pltpu.roll(v[:S].astype(F32), S - 1, 0)
    ref[at + (slice(0, S), slice(0, C))] = jnp.where(spot == 0, 0.0, last).astype(BF)
    ref[at + (slice(S + W, E), slice(0, C))] = jnp.where(spot == S - 1, 0.0, head).astype(BF)


def taps(src, todo, w, par):
    acc = jnp.zeros((W, C), F32)
    for t, v, a, p in todo:
        for q in range(3):
            wt = w[a, p + par * (2 - 2 * p), q]
            acc = acc + jnp.dot(src[t, v, S * q : S * q + W, :], wt, preferred_element_type=F32)
    return acc


def here():
    r = lax.axis_index("rows")
    keep = jnp.where((r == 0) | (r == lax.axis_size("rows") - 1), 0.0, 1.0).astype(F32)
    return r % 2, keep


def prep_kernel(x_hbm, g_hbm, own_ref, b_ref, a_ref, t_ref, d_ref, x_ref, g_ref, sem):
    par, _ = here()
    cg = pltpu.make_async_copy(g_hbm, g_ref, sem.at[4])
    cg.start()
    copies = [pltpu.make_async_copy(x_hbm.at[t], x_ref.at[t], sem.at[t]) for t in range(4)]
    for c in copies:
        c.start()
    m = spread(E, 1)
    cg.wait()
    g = g_ref[...]
    for t in range(4):
        copies[t].wait()
        for u in range(4):
            xp = jnp.dot(m, x_ref[t, flip(u, par)], preferred_element_type=F32)
            f = act(xp, g).astype(BF)
            own_ref[t, u] = f
            d = pack(f[S : S + W])
            if u < 2:
                b_ref[t, u] = d
                if t >= 2:
                    d_ref[t - 2, u] = d
            else:
                a_ref[t, 3 - u] = d
            if t >= 2:
                t_ref[t - 2, u] = d


def early_kernel(own_ref, a_ref, w1_ref, w2_ref, b_ref, g_ref, s_ref, o_ref, i_ref, pe_ref, pf_ref, x_ref):
    par, _ = here()
    for t in range(4):
        for u in range(4):
            x_ref[t, u] = own_ref[t, u]
        for k in range(2):
            put(x_ref, (t, 4 + k), unpack(a_ref[t, k]))
    bias = b_ref[...]
    g = g_ref[...]

    def row(k, _):
        for tau in range(2):
            acc = taps(x_ref, [(tau + a, k + p, a, p) for a in range(3) for p in range(3)], w1_ref, par)
            put(s_ref, (tau, k), act(acc + bias, g).astype(BF))
        o_ref[0, k] = taps(x_ref, [(0, k + p, 2, p) for p in range(3)], w1_ref, par)
        o_ref[1, k] = taps(x_ref, [(a - 1, k + p, a, p) for a in (1, 2) for p in range(3)], w1_ref, par)
        return 0

    lax.fori_loop(0, 4, row, 0)
    for tau in range(4):
        ok = [a for a in range(3) if tau + a >= 2]
        i_ref[tau, 0] = taps(x_ref, [(tau + a - 2, 0, a, 2) for a in ok], w1_ref, par)
        i_ref[tau, 1] = taps(x_ref, [(tau + a - 2, p - 1, a, p) for a in ok for p in (1, 2)], w1_ref, par)
    for tau in range(2):
        ok = range(2 - tau)
        pf_ref[tau, 0] = taps(s_ref, [(tau + a, 0, a, 2) for a in ok], w2_ref, par)
        pf_ref[tau, 1] = taps(s_ref, [(tau + a, p - 1, a, p) for a in ok for p in (1, 2)], w2_ref, par)
        for u in range(2):
            acc = taps(s_ref, [(tau + a, u + p, a, p) for a in ok for p in range(3)], w2_ref, par)
            pe_ref[tau, u] = pack(acc.astype(BF))


def mid_kernel(bx_ref, i_ref, pe_ref, pf_ref, w1_ref, w2_ref, b_ref, g_ref, s_ref, p_ref, x_ref):
    par, keep = here()
    for t in range(4):
        for k in range(2):
            put(x_ref, (t, 1 - k), unpack(bx_ref[t, k]))
    bias = b_ref[...]
    g = g_ref[...]
    for tau in range(2):
        acc = taps(x_ref, [(tau + a, p, a, p) for a in range(3) for p in range(2)], w1_ref, par)
        put(s_ref, (tau, 0), (act(acc + i_ref[tau + 2, 0] + bias, g) * keep).astype(BF))
        acc = taps(x_ref, [(tau + a, 1, a, 0) for a in range(3)], w1_ref, par)
        put(s_ref, (tau, 1), act(acc + i_ref[tau + 2, 1] + bias, g).astype(BF))
    for tau in range(2):
        for u in range(2):
            p_ref[tau, u + 2] = pe_ref[tau, u]
        ok = range(2 - tau)
        acc = taps(s_ref, [(tau + a, p, a, p) for a in ok for p in range(2)], w2_ref, par)
        p_ref[tau, 0] = pack((acc + pf_ref[tau, 0]).astype(BF))
        acc = taps(s_ref, [(tau + a, 1, a, 0) for a in ok], w2_ref, par)
        p_ref[tau, 1] = pack((acc + pf_ref[tau, 1]).astype(BF))


def wait_kernel(bx_ref, i_ref, se_ref, sm_ref, w1_ref, w2_ref, j_ref, z_ref, x_ref, s_ref):
    par, _ = here()
    for t in range(2):
        for k in range(2):
            put(x_ref, (t, 1 - k), unpack(bx_ref[t, k]))
            s_ref[t, k] = sm_ref[t, k]
        for k in range(4):
            s_ref[t, k + 2] = se_ref[t, k]
    for tau in range(2):
        ok = [a for a in range(3) if tau + a >= 2]
        acc = taps(x_ref, [(tau + a - 2, p, a, p) for a in ok for p in range(2)], w1_ref, par)
        j_ref[tau, 0] = acc + i_ref[tau, 0]
        acc = taps(x_ref, [(tau + a - 2, 1, a, 0) for a in ok], w1_ref, par)
        j_ref[tau, 1] = acc + i_ref[tau, 1]

    def row(u, _):
        z_ref[0, u] = taps(s_ref, [(0, u + p, 2, p) for p in range(3)], w2_ref, par)
        z_ref[1, u] = taps(s_ref, [(a - 1, u + p, a, p) for a in (1, 2) for p in range(3)], w2_ref, par)
        return 0

    lax.fori_loop(0, 4, row, 0)


def late_kernel(
    t_ref, d_ref, c_ref, o_ref, j_ref, z_ref, w1_ref, w2_ref, b_ref, g_ref, b2_ref, in_ref,
    out_ref, acc_ref, x_ref, s_ref, i_ref, y_ref,
):
    par, keep = here()
    for t in range(2):
        for u in range(4):
            put(x_ref, (t, u + 2), unpack(t_ref[t, u]))
        for k in range(2):
            put(x_ref, (t, 1 - k), unpack(d_ref[t, k]))
            put(x_ref, (t, 6 + k), unpack(c_ref[t, k]))
            i_ref[t, k] = j_ref[t, k]
        for k in range(4):
            i_ref[t, k + 2] = o_ref[t, k]
    bias = b_ref[...]
    g = g_ref[...]

    def row(v, _):
        hold = jnp.where(v == 0, keep, 1.0)
        for tau in range(2):
            acc = taps(x_ref, [(tau + a, v + p, a, p) for a in range(2 - tau) for p in range(3)], w1_ref, par)
            put(s_ref, (tau, v), (act(acc + i_ref[tau, v] + bias, g) * hold).astype(BF))
        return 0

    lax.fori_loop(0, 6, row, 0)
    bias2 = b2_ref[...]
    m = spread(W, 0)

    def last(u, _):
        at = flip(u, par)
        for tau in range(4):
            start = jnp.dot(m, in_ref[tau, at], preferred_element_type=F32) + bias2
            frames = [f for f in range(2) if 0 <= f - tau + 2 <= 2]
            acc = taps(s_ref, [(f, u + p, f - tau + 2, p) for f in frames for p in range(3)], w2_ref, par)
            if tau < 2:
                acc_ref[tau, u] = acc + start
            else:
                y_ref[tau - 2, u] = (acc + z_ref[tau - 2, u] + start).astype(BF)
        return 0

    lax.fori_loop(0, 4, last, 0)
    back = gather()
    for tau in range(2):
        for u in range(4):
            y = jnp.dot(back, y_ref[tau, u], preferred_element_type=F32)
            out_ref[tau + 2, flip(u, par)] = y.astype(BF)


def add_kernel(acc_ref, p_ref, full_ref, out_ref):
    par, _ = here()
    back = gather()
    for u in range(4):
        y = (acc_ref[0, u] + unpack(p_ref[0, u]).astype(F32)).astype(BF)
        z = jnp.dot(back, y, preferred_element_type=F32)
        out_ref[0, flip(u, par)] = z.astype(BF)


VMEM = pl.BlockSpec(memory_space=pltpu.VMEM)
HBM = pl.BlockSpec(memory_space=pltpu.HBM)


def call(kernel, name, ins, outs, scratch, units, limit=32, in_specs=None):
    return pl.pallas_call(
        kernel,
        in_specs=in_specs or [VMEM] * len(ins),
        out_specs=[VMEM] * len(outs),
        out_shape=[jax.ShapeDtypeStruct(s, d) for s, d in outs],
        scratch_shapes=scratch,
        compiler_params=pltpu.CompilerParams(vmem_limit_bytes=limit * MB),
        cost_estimate=pl.CostEstimate(
            flops=int(units * 6e8), bytes_accessed=3_000_000, transcendentals=500_000
        ),
        name=name,
    )(*ins)


def local(frames_in, gain_one, conv_one, bias_one, gain_two, conv_two, bias_two):
    n = lax.axis_size("rows")
    near = [(i, i ^ 1) for i in range(n)]
    far = [(i, i + 1) for i in range(1, n - 1, 2)] + [(i + 1, i) for i in range(1, n - 1, 2)]
    diag = [(i, n + j) for i, j in far]
    g1, g2 = gain_one.reshape(1, C), gain_two.reshape(1, C)
    b1, b2 = bias_one.reshape(1, C), bias_two.reshape(1, C)

    own, bs, as_, ts, ds = call(
        prep_kernel, "prep", [frames_in, g1],
        [((4, 4, E, C), BF), ((4, 2, D, 128), BF), ((4, 2, D, 128), BF), ((2, 4, D, 128), BF), ((2, 2, D, 128), BF)],
        [pltpu.VMEM((4, 4, W, C), BF), pltpu.VMEM((1, C), F32), pltpu.SemaphoreType.DMA((5,))],
        1, in_specs=[HBM, HBM],
    )
    ar = lax.ppermute(as_, "rows", near)
    br = lax.ppermute(bs, "rows", far)
    ts, ds, ar = lax.optimization_barrier((ts, ds, ar))
    tr = lax.ppermute(ts, "tm", [(0, 1)])
    dr = lax.ppermute(ds, ("tm", "rows"), diag)

    se, oacc, iacc, pe, pf = call(
        early_kernel, "early", [own, ar, conv_one, conv_two, b1, g2],
        [((2, 4, E, C), BF), ((2, 4, W, C), F32), ((4, 2, W, C), F32), ((2, 2, D, 128), BF), ((2, 2, W, C), F32)],
        [pltpu.VMEM((4, 6, E, C), BF)], 18,
    )
    sm, ps = call(
        mid_kernel, "mid", [br, iacc, pe, pf, conv_one, conv_two, b1, g2],
        [((2, 2, E, C), BF), ((2, 4, D, 128), BF)],
        [pltpu.VMEM((4, 2, E, C), BF)], 3,
    )
    pr = lax.ppermute(ps, "tm", [(0, 1)])
    jacc, zacc = call(
        wait_kernel, "wait", [br, iacc, se, sm, conv_one, conv_two],
        [((2, 2, W, C), F32), ((2, 4, W, C), F32)],
        [pltpu.VMEM((2, 2, E, C), BF), pltpu.VMEM((2, 6, E, C), BF)], 5,
    )
    tr, dr, ps = lax.optimization_barrier((tr, dr, ps))
    cr = lax.ppermute(jnp.stack([tr[:, 3], tr[:, 2]], axis=1), "rows", near)
    out, acc = call(
        late_kernel, "late", [tr, dr, cr, oacc, jacc, zacc, conv_one, conv_two, b1, g2, b2, frames_in],
        [((4, 4, W, C), BF), ((2, 4, W, C), F32)],
        [pltpu.VMEM((2, 8, E, C), BF), pltpu.VMEM((2, 6, E, C), BF), pltpu.VMEM((2, 6, W, C), F32), pltpu.VMEM((2, 4, W, C), BF)],
        14,
    )
    return pl.pallas_call(
        add_kernel,
        grid=(2,),
        in_specs=[
            pl.BlockSpec((1, 4, W, C), lambda t: (t, 0, 0, 0)),
            pl.BlockSpec((1, 4, D, 128), lambda t: (t, 0, 0, 0)),
            pl.BlockSpec(memory_space=pl.ANY),
        ],
        out_specs=pl.BlockSpec((1, 4, W, C), lambda t: (t, 0, 0, 0)),
        out_shape=jax.ShapeDtypeStruct((4, 4, W, C), BF),
        input_output_aliases={2: 0},
        compiler_params=pltpu.CompilerParams(vmem_limit_bytes=24 * MB),
        cost_estimate=pl.CostEstimate(flops=600_000_000, bytes_accessed=3_000_000, transcendentals=0),
        name="add",
    )(acc, pr, out)


def solution(mesh):
    in_specs = (P("tm", "rows", "roll", None), P(), P(), P(), P(), P(), P())
    out_specs = P("tm", "rows", "roll", None)
    return jax.shard_map(local, mesh=mesh, in_specs=in_specs, out_specs=out_specs, check_vma=False)
```

```python
import jax
import jax.numpy as jnp
from jax import lax
from jax.experimental import pallas as pl
from jax.experimental.pallas import tpu as pltpu
from jax.sharding import PartitionSpec as P

BF = jnp.bfloat16
F32 = jnp.float32
C = 192
W = 160
S = 16
J = W // S
E = W + 2 * S
D = 240
MB = 2**20


def spread(rows, shift):
    n = lax.broadcasted_iota(jnp.int32, (rows, W), 0)
    c = lax.broadcasted_iota(jnp.int32, (rows, W), 1)
    return jnp.where((n & (S - 1)) * J + (n >> 4) - shift == c, 1.0, 0.0).astype(BF)


def gather():
    c = lax.broadcasted_iota(jnp.int32, (W, W), 0)
    n = lax.broadcasted_iota(jnp.int32, (W, W), 1)
    return jnp.where((n & (S - 1)) * J + (n >> 4) == c, 1.0, 0.0).astype(BF)


def flip(n, par):
    return n + par * (3 - 2 * n)


def act(v, gain):
    power = jnp.mean(v * v, axis=-1, keepdims=True)
    h = v * lax.rsqrt(power + 1e-06) * (gain * 0.5)
    return h + h * jnp.tanh(h)


def pack(v):
    hi = v[:, 128:]
    return jnp.concatenate([v[:, :128], jnp.concatenate([hi[:80], hi[80:]], axis=1)], axis=0)


def unpack(d):
    hi = d[W:]
    return jnp.concatenate([d[:W], jnp.concatenate([hi[:, :64], hi[:, 64:]], axis=0)], axis=1)


def put(ref, at, v):
    ref[at + (slice(S, S + W), slice(0, C))] = v
    spot = lax.broadcasted_iota(jnp.int32, (S, C), 0)
    last = pltpu.roll(v[W - S :].astype(F32), 1, 0)
    head = pltpu.roll(v[:S].astype(F32), S - 1, 0)
    ref[at + (slice(0, S), slice(0, C))] = jnp.where(spot == 0, 0.0, last).astype(BF)
    ref[at + (slice(S + W, E), slice(0, C))] = jnp.where(spot == S - 1, 0.0, head).astype(BF)


def taps(src, todo, w, par):
    acc = jnp.zeros((W, C), F32)
    for t, v, a, p in todo:
        for q in range(3):
            wt = w[a, p + par * (2 - 2 * p), q]
            acc = acc + jnp.dot(src[t, v, S * q : S * q + W, :], wt, preferred_element_type=F32)
    return acc


def here():
    r = lax.axis_index("rows")
    keep = jnp.where((r == 0) | (r == lax.axis_size("rows") - 1), 0.0, 1.0).astype(F32)
    return r % 2, keep


def prep_kernel(x_ref, k_ref, own_ref, b_ref, a_ref, t_ref, d_ref):
    par, _ = here()
    m = spread(E, 1)
    g = k_ref[0:1, :]
    for t in range(4):
        for u in range(4):
            xp = jnp.dot(m, x_ref[t, flip(u, par)], preferred_element_type=F32)
            f = act(xp, g).astype(BF)
            own_ref[t, u] = f
            d = pack(f[S : S + W])
            if u < 2:
                b_ref[t, u] = d
                if t >= 2:
                    d_ref[t - 2, u] = d
            else:
                a_ref[t, 3 - u] = d
            if t >= 2:
                t_ref[t - 2, u] = d


def early_kernel(own_ref, a_ref, w1_ref, w2_ref, k_ref, s_ref, o_ref, i_ref, pe_ref, pf_ref, x_ref):
    par, _ = here()
    for t in range(4):
        for u in range(4):
            x_ref[t, u] = own_ref[t, u]
        for k in range(2):
            put(x_ref, (t, 4 + k), unpack(a_ref[t, k]))
    bias, g = k_ref[1:2, :], k_ref[2:3, :]

    def row(k, _):
        for tau in range(2):
            acc = taps(x_ref, [(tau + a, k + p, a, p) for a in range(3) for p in range(3)], w1_ref, par)
            put(s_ref, (tau, k), act(acc + bias, g).astype(BF))
        o_ref[0, k] = taps(x_ref, [(0, k + p, 2, p) for p in range(3)], w1_ref, par)
        o_ref[1, k] = taps(x_ref, [(a - 1, k + p, a, p) for a in (1, 2) for p in range(3)], w1_ref, par)
        return 0

    lax.fori_loop(0, 4, row, 0)
    for tau in range(4):
        ok = [a for a in range(3) if tau + a >= 2]
        i_ref[tau, 0] = taps(x_ref, [(tau + a - 2, 0, a, 2) for a in ok], w1_ref, par)
        i_ref[tau, 1] = taps(x_ref, [(tau + a - 2, p - 1, a, p) for a in ok for p in (1, 2)], w1_ref, par)
    for tau in range(2):
        ok = range(2 - tau)
        pf_ref[tau, 0] = taps(s_ref, [(tau + a, 0, a, 2) for a in ok], w2_ref, par)
        pf_ref[tau, 1] = taps(s_ref, [(tau + a, p - 1, a, p) for a in ok for p in (1, 2)], w2_ref, par)
        for u in range(2):
            acc = taps(s_ref, [(tau + a, u + p, a, p) for a in ok for p in range(3)], w2_ref, par)
            pe_ref[tau, u] = pack(acc.astype(BF))


def mid_kernel(bx_ref, i_ref, pe_ref, pf_ref, w1_ref, w2_ref, k_ref, s_ref, p_ref, x_ref):
    par, keep = here()
    for t in range(4):
        for k in range(2):
            put(x_ref, (t, 1 - k), unpack(bx_ref[t, k]))
    bias, g = k_ref[1:2, :], k_ref[2:3, :]
    for tau in range(2):
        acc = taps(x_ref, [(tau + a, p, a, p) for a in range(3) for p in range(2)], w1_ref, par)
        put(s_ref, (tau, 0), (act(acc + i_ref[tau + 2, 0] + bias, g) * keep).astype(BF))
        acc = taps(x_ref, [(tau + a, 1, a, 0) for a in range(3)], w1_ref, par)
        put(s_ref, (tau, 1), act(acc + i_ref[tau + 2, 1] + bias, g).astype(BF))
    for tau in range(2):
        for u in range(2):
            p_ref[tau, u + 2] = pe_ref[tau, u]
        ok = range(2 - tau)
        acc = taps(s_ref, [(tau + a, p, a, p) for a in ok for p in range(2)], w2_ref, par)
        p_ref[tau, 0] = pack((acc + pf_ref[tau, 0]).astype(BF))
        acc = taps(s_ref, [(tau + a, 1, a, 0) for a in ok], w2_ref, par)
        p_ref[tau, 1] = pack((acc + pf_ref[tau, 1]).astype(BF))


def wait_kernel(bx_ref, i_ref, se_ref, sm_ref, w1_ref, w2_ref, j_ref, z_ref, x_ref, s_ref):
    par, _ = here()
    for t in range(2):
        for k in range(2):
            put(x_ref, (t, 1 - k), unpack(bx_ref[t, k]))
            s_ref[t, k] = sm_ref[t, k]
        for k in range(4):
            s_ref[t, k + 2] = se_ref[t, k]
    for tau in range(2):
        ok = [a for a in range(3) if tau + a >= 2]
        acc = taps(x_ref, [(tau + a - 2, p, a, p) for a in ok for p in range(2)], w1_ref, par)
        j_ref[tau, 0] = acc + i_ref[tau, 0]
        acc = taps(x_ref, [(tau + a - 2, 1, a, 0) for a in ok], w1_ref, par)
        j_ref[tau, 1] = acc + i_ref[tau, 1]

    def row(u, _):
        z_ref[0, u] = taps(s_ref, [(0, u + p, 2, p) for p in range(3)], w2_ref, par)
        z_ref[1, u] = taps(s_ref, [(a - 1, u + p, a, p) for a in (1, 2) for p in range(3)], w2_ref, par)
        return 0

    lax.fori_loop(0, 4, row, 0)


def late_kernel(
    t_ref, d_ref, c_ref, o_ref, j_ref, z_ref, w1_ref, w2_ref, k_ref, in_ref,
    out_ref, acc_ref, x_ref, s_ref, y_ref, n_ref, sem,
):
    par, keep = here()

    def fetch(v):
        for t in range(2):
            d = d_ref[t, 1 - v] if v < 2 else t_ref[t, v - 2] if v < 6 else c_ref[t, v - 6]
            put(x_ref, (t, v), unpack(d))

    for v in range(3):
        fetch(v)
    bias, g, bias2 = k_ref[1:2, :], k_ref[2:3, :], k_ref[3:4, :]
    for v in range(6):
        if v:
            fetch(v + 2)
        for tau in range(2):
            acc = taps(x_ref, [(tau + a, v + p, a, p) for a in range(2 - tau) for p in range(3)], w1_ref, par)
            f = act(acc + (j_ref[tau, v] if v < 2 else o_ref[tau, v - 2]) + bias, g)
            put(s_ref, (tau, v), (f if v else f * keep).astype(BF))
    m, back = spread(W, 0), gather()

    def leave(tau, u):
        return pltpu.make_async_copy(n_ref.at[tau, u], out_ref.at[tau + 2, flip(u, par)], sem.at[tau, u])

    def finish(u):
        for tau in range(2):
            n_ref[tau, u] = jnp.dot(back, y_ref[tau, u], preferred_element_type=F32).astype(BF)
            leave(tau, u).start()

    for u in range(4):
        at = flip(u, par)
        for tau in range(4):
            start = jnp.dot(m, in_ref[tau, at], preferred_element_type=F32) + bias2
            frames = [f for f in range(2) if 0 <= f - tau + 2 <= 2]
            acc = taps(s_ref, [(f, u + p, f - tau + 2, p) for f in frames for p in range(3)], w2_ref, par)
            if tau < 2:
                acc_ref[tau, u] = acc + start
            else:
                y_ref[tau - 2, u] = (acc + z_ref[tau - 2, u] + start).astype(BF)
        if u:
            finish(u - 1)
    finish(3)
    for u in range(4):
        for tau in range(2):
            leave(tau, u).wait()


def add_kernel(acc_ref, p_ref, full_ref, out_ref, n_ref, sem):
    par, _ = here()
    back = gather()
    sent = []
    for t in range(2):
        for u in range(4):
            y = (acc_ref[t, u] + unpack(p_ref[t, u]).astype(F32)).astype(BF)
            n_ref[t, u] = jnp.dot(back, y, preferred_element_type=F32).astype(BF)
            copy = pltpu.make_async_copy(n_ref.at[t, u], out_ref.at[t, flip(u, par)], sem.at[t, u])
            copy.start()
            sent.append(copy)
    for copy in sent:
        copy.wait()


VMEM = pl.BlockSpec(memory_space=pltpu.VMEM)
ANY = pl.BlockSpec(memory_space=pl.ANY)


def call(kernel, name, ins, outs, scratch, units, limit=32, in_specs=None, out_specs=None, alias={}):
    return pl.pallas_call(
        kernel,
        in_specs=in_specs or [VMEM] * len(ins),
        out_specs=out_specs or [VMEM] * len(outs),
        out_shape=[jax.ShapeDtypeStruct(s, d) for s, d in outs],
        scratch_shapes=scratch,
        compiler_params=pltpu.CompilerParams(vmem_limit_bytes=limit * MB),
        cost_estimate=pl.CostEstimate(
            flops=int(units * 6e8), bytes_accessed=3_000_000, transcendentals=500_000
        ),
        input_output_aliases=alias,
        name=name,
    )(*ins)


def local(frames_in, gain_one, conv_one, bias_one, gain_two, conv_two, bias_two):
    n = lax.axis_size("rows")
    near = [(i, i ^ 1) for i in range(n)]
    far = [(i, i + 1) for i in range(1, n - 1, 2)] + [(i + 1, i) for i in range(1, n - 1, 2)]
    diag = [(i, n + j) for i, j in far]
    kv = jnp.stack([gain_one, bias_one, gain_two, bias_two])

    own, bs, as_, ts, ds = call(
        prep_kernel, "prep", [frames_in, kv],
        [((4, 4, E, C), BF), ((4, 2, D, 128), BF), ((4, 2, D, 128), BF), ((2, 4, D, 128), BF), ((2, 2, D, 128), BF)],
        [], 40,
    )
    ar = lax.ppermute(as_, "rows", near)
    br = lax.ppermute(bs, "rows", far)
    ts, ds, ar = lax.optimization_barrier((ts, ds, ar))
    tr = lax.ppermute(ts, "tm", [(0, 1)])
    dr = lax.ppermute(ds, ("tm", "rows"), diag)

    se, oacc, iacc, pe, pf = call(
        early_kernel, "early", [own, ar, conv_one, conv_two, kv],
        [((2, 4, E, C), BF), ((2, 4, W, C), F32), ((4, 2, W, C), F32), ((2, 2, D, 128), BF), ((2, 2, W, C), F32)],
        [pltpu.VMEM((4, 6, E, C), BF)], 18,
    )
    sm, ps = call(
        mid_kernel, "mid", [br, iacc, pe, pf, conv_one, conv_two, kv],
        [((2, 2, E, C), BF), ((2, 4, D, 128), BF)],
        [pltpu.VMEM((4, 2, E, C), BF)], 3,
    )
    pr = lax.ppermute(ps, "tm", [(0, 1)])
    jacc, zacc = call(
        wait_kernel, "wait", [br, iacc, se, sm, conv_one, conv_two],
        [((2, 2, W, C), F32), ((2, 4, W, C), F32)],
        [pltpu.VMEM((2, 2, E, C), BF), pltpu.VMEM((2, 6, E, C), BF)], 20,
    )
    tr, dr, zacc = lax.optimization_barrier((tr, dr, zacc))
    cr = lax.ppermute(jnp.stack([tr[:, 3], tr[:, 2]], axis=1), "rows", near)
    out, acc = call(
        late_kernel, "late", [tr, dr, cr, oacc, jacc, zacc, conv_one, conv_two, kv, frames_in],
        [((4, 4, W, C), BF), ((2, 4, W, C), F32)],
        [
            pltpu.VMEM((2, 8, E, C), BF), pltpu.VMEM((2, 6, E, C), BF), pltpu.VMEM((2, 4, W, C), BF),
            pltpu.VMEM((2, 4, W, C), BF), pltpu.SemaphoreType.DMA((2, 4)),
        ],
        1, out_specs=[ANY, VMEM],
    )
    (out,) = call(
        add_kernel, "add", [acc, pr, out], [((4, 4, W, C), BF)],
        [pltpu.VMEM((2, 4, W, C), BF), pltpu.SemaphoreType.DMA((2, 4))],
        1, in_specs=[VMEM, VMEM, ANY], out_specs=[ANY], alias={2: 0},
    )
    return out


def solution(mesh):
    in_specs = (P("tm", "rows", "roll", None), P(), P(), P(), P(), P(), P())
    out_specs = P("tm", "rows", "roll", None)
    return jax.shard_map(local, mesh=mesh, in_specs=in_specs, out_specs=out_specs, check_vma=False)
```

```python
import jax
import jax.numpy as jnp
from jax import lax
from jax.experimental import pallas as pl
from jax.experimental.pallas import tpu as pltpu
from jax.sharding import PartitionSpec as P

BF = jnp.bfloat16
F32 = jnp.float32
C = 192
W = 160
S = 16
J = W // S
E = W + 2 * S
D = 240
MB = 2**20


def spread(rows, shift):
    n = lax.broadcasted_iota(jnp.int32, (rows, W), 0)
    c = lax.broadcasted_iota(jnp.int32, (rows, W), 1)
    return jnp.where((n & (S - 1)) * J + (n >> 4) - shift == c, 1.0, 0.0).astype(BF)


def gather():
    c = lax.broadcasted_iota(jnp.int32, (W, W), 0)
    n = lax.broadcasted_iota(jnp.int32, (W, W), 1)
    return jnp.where((n & (S - 1)) * J + (n >> 4) == c, 1.0, 0.0).astype(BF)


def flip(n, par):
    return n + par * (3 - 2 * n)


def act(v, gain):
    power = jnp.mean(v * v, axis=-1, keepdims=True)
    h = v * lax.rsqrt(power + 1e-06) * (gain * 0.5)
    return h + h * jnp.tanh(h)


def pack(v):
    hi = v[:, 128:]
    return jnp.concatenate([v[:, :128], jnp.concatenate([hi[:80], hi[80:]], axis=1)], axis=0)


def unpack(d):
    hi = d[W:]
    return jnp.concatenate([d[:W], jnp.concatenate([hi[:, :64], hi[:, 64:]], axis=0)], axis=1)


def edged(v):
    spot = lax.broadcasted_iota(jnp.int32, (S, C), 0)
    last = pltpu.roll(v[W - S :].astype(F32), 1, 0)
    head = pltpu.roll(v[:S].astype(F32), S - 1, 0)
    last = jnp.where(spot == 0, 0.0, last).astype(BF)
    head = jnp.where(spot == S - 1, 0.0, head).astype(BF)
    return jnp.concatenate([last, v, head], axis=0)


def place(ref, t, v, full, above=True):
    hi = full[:, 128:]
    ref[t, v, 0] = full[:, :128]
    on = jnp.concatenate([hi[S:], jnp.zeros((S, C - 128), BF)], axis=0)
    ref[t, v, 1] = jnp.concatenate([hi, on], axis=1)
    ref[t, v, 2, :, 0:64] = hi
    if above:
        ref[t, v - 1, 2, :, 64:128] = hi


def put(ref, at, v, above=True):
    place(ref, at[0], at[1], edged(v), above)


def taps(src, todo, w, par):
    ins, wts = [], []
    for t, v, a, ps in todo:
        at = {p: p + par * (2 - 2 * p) for p in ps}
        for p in ps:
            for q in range(3):
                ins.append(src[t, v + p, 0, S * q : S * q + W, :])
                wts.append(w[a, at[p], q, 0:128, :])
            ins.append(src[t, v + p, 1, 0:W, :])
            wts.append(jnp.concatenate([w[a, at[p], q, 128:C, :] for q in range(2)], axis=0))
        ps = list(ps)
        while ps:
            p = ps.pop(0)
            if ps:
                more = w[a, at[ps.pop(0)], 2, 128:C, :]
                ins.append(src[t, v + p, 2, 2 * S : E, :])
            else:
                more = jnp.zeros((C - 128, C), BF)
                ins.append(src[t, v + p, 1, 2 * S : E, :])
            wts.append(jnp.concatenate([w[a, at[p], 2, 128:C, :], more], axis=0))
    acc = jnp.zeros((W, C), F32)
    for i in range(0, len(ins), 2):
        left = jnp.concatenate(ins[i : i + 2], axis=1)
        right = jnp.concatenate(wts[i : i + 2], axis=0)
        acc = acc + jnp.dot(left, right, preferred_element_type=F32)
    return acc


def here():
    r = lax.axis_index("rows")
    keep = jnp.where((r == 0) | (r == lax.axis_size("rows") - 1), 0.0, 1.0).astype(F32)
    return r % 2, keep


def prep_kernel(x_ref, k_ref, own_ref, b_ref, a_ref, t_ref, d_ref):
    par, _ = here()
    m = spread(E, 1)
    g = k_ref[0:1, :]
    for t in range(4):
        for u in range(4):
            xp = jnp.dot(m, x_ref[t, flip(u, par)], preferred_element_type=F32)
            f = act(xp, g).astype(BF)
            own_ref[t, u, 0] = f[:, :128]
            hi = f[:, 128:]
            on = jnp.concatenate([hi[S:], jnp.zeros((S, C - 128), BF)], axis=0)
            own_ref[t, u, 1] = jnp.concatenate([hi, on], axis=1)
            own_ref[t, u, 2, :, 0:64] = hi
            if u:
                own_ref[t, u - 1, 2, :, 64:128] = hi
            d = pack(f[S : S + W])
            if u < 2:
                b_ref[t, u] = d
                if t >= 2:
                    d_ref[t - 2, u] = d
            else:
                a_ref[t, 3 - u] = d
            if t >= 2:
                t_ref[t - 2, u] = d


def early_kernel(own_ref, a_ref, w1_ref, w2_ref, k_ref, r_ref, o_ref, i_ref, pe_ref, pf_ref, x_ref, s_ref):
    par, _ = here()
    for t in range(4):
        for u in range(4):
            x_ref[t, u] = own_ref[t, u]
        for k in range(2):
            put(x_ref, (t, 4 + k), unpack(a_ref[t, k]))
    bias, g = k_ref[1:2, :], k_ref[2:3, :]
    all3 = (0, 1, 2)

    def row(k, _):
        for tau in range(2):
            acc = taps(x_ref, [(tau + a, k, a, all3) for a in range(3)], w1_ref, par)
            f = act(acc + bias, g).astype(BF)
            r_ref[tau, k] = f
            put(s_ref, (tau, k + 1), f)
        o_ref[0, k] = taps(x_ref, [(0, k, 2, all3)], w1_ref, par)
        o_ref[1, k] = taps(x_ref, [(a - 1, k, a, all3) for a in (1, 2)], w1_ref, par)
        return 0

    lax.fori_loop(0, 4, row, 0)
    for tau in range(4):
        ok = [a for a in range(3) if tau + a >= 2]
        i_ref[tau, 0] = taps(x_ref, [(tau + a - 2, -2, a, (2,)) for a in ok], w1_ref, par)
        i_ref[tau, 1] = taps(x_ref, [(tau + a - 2, -1, a, (1, 2)) for a in ok], w1_ref, par)
    for tau in range(2):
        ok = range(2 - tau)
        pf_ref[tau, 0] = taps(s_ref, [(tau + a, -1, a, (2,)) for a in ok], w2_ref, par)
        pf_ref[tau, 1] = taps(s_ref, [(tau + a, 0, a, (1, 2)) for a in ok], w2_ref, par)
        for u in range(2):
            acc = taps(s_ref, [(tau + a, u + 1, a, all3) for a in ok], w2_ref, par)
            pe_ref[tau, u] = pack(acc.astype(BF))


def mid_kernel(bx_ref, i_ref, pe_ref, pf_ref, w1_ref, w2_ref, k_ref, r_ref, p_ref, x_ref, s_ref):
    par, keep = here()
    for t in range(4):
        for k in (1, 0):
            put(x_ref, (t, 1 - k), unpack(bx_ref[t, k]), above=k == 0)
    bias, g = k_ref[1:2, :], k_ref[2:3, :]
    for tau in range(2):
        acc = taps(x_ref, [(tau + a, 0, a, (0, 1)) for a in range(3)], w1_ref, par)
        r_ref[tau, 0] = (act(acc + i_ref[tau + 2, 0] + bias, g) * keep).astype(BF)
        acc = taps(x_ref, [(tau + a, 1, a, (0,)) for a in range(3)], w1_ref, par)
        r_ref[tau, 1] = act(acc + i_ref[tau + 2, 1] + bias, g).astype(BF)
        for v in range(2):
            put(s_ref, (tau, v), r_ref[tau, v], above=v > 0)
    for tau in range(2):
        for u in range(2):
            p_ref[tau, u + 2] = pe_ref[tau, u]
        ok = range(2 - tau)
        acc = taps(s_ref, [(tau + a, 0, a, (0, 1)) for a in ok], w2_ref, par)
        p_ref[tau, 0] = pack((acc + pf_ref[tau, 0]).astype(BF))
        acc = taps(s_ref, [(tau + a, 1, a, (0,)) for a in ok], w2_ref, par)
        p_ref[tau, 1] = pack((acc + pf_ref[tau, 1]).astype(BF))


def wait_kernel(bx_ref, i_ref, re_ref, rm_ref, w1_ref, w2_ref, k_ref, in_ref, j_ref, z_ref, x_ref, s_ref):
    par, _ = here()
    for t in range(2):
        for k in (1, 0):
            put(x_ref, (t, 1 - k), unpack(bx_ref[t, k]), above=k == 0)
        for v in range(6):
            put(s_ref, (t, v), rm_ref[t, v] if v < 2 else re_ref[t, v - 2], above=v > 0)
    for tau in range(2):
        ok = [a for a in range(3) if tau + a >= 2]
        acc = taps(x_ref, [(tau + a - 2, 0, a, (0, 1)) for a in ok], w1_ref, par)
        j_ref[tau, 0] = acc + i_ref[tau, 0]
        acc = taps(x_ref, [(tau + a - 2, 1, a, (0,)) for a in ok], w1_ref, par)
        j_ref[tau, 1] = acc + i_ref[tau, 1]
    bias2 = k_ref[3:4, :]
    m = spread(W, 0)

    def row(u, _):
        at = flip(u, par)
        for tau in range(4):
            start = jnp.dot(m, in_ref[tau, at], preferred_element_type=F32) + bias2
            if tau >= 2:
                todo = [(f, u, f - tau + 4, (0, 1, 2)) for f in range(tau - 1)]
                start = start + taps(s_ref, todo, w2_ref, par)
            z_ref[tau, u] = start
        return 0

    lax.fori_loop(0, 4, row, 0)


def late_kernel(
    t_ref, d_ref, c_ref, o_ref, j_ref, z_ref, w1_ref, w2_ref, k_ref,
    out_ref, acc_ref, x_ref, s_ref, y_ref, n_ref, sem,
):
    par, keep = here()

    def fetch(v):
        for t in range(2):
            d = d_ref[t, 1 - v] if v < 2 else t_ref[t, v - 2] if v < 6 else c_ref[t, v - 6]
            put(x_ref, (t, v), unpack(d), above=v > 0)

    for v in range(3):
        fetch(v)
    bias, g = k_ref[1:2, :], k_ref[2:3, :]
    for v in range(6):
        if v:
            fetch(v + 2)
        for tau in range(2):
            acc = taps(x_ref, [(tau + a, v, a, (0, 1, 2)) for a in range(2 - tau)], w1_ref, par)
            f = act(acc + (j_ref[tau, v] if v < 2 else o_ref[tau, v - 2]) + bias, g)
            put(s_ref, (tau, v), (f if v else f * keep).astype(BF), above=v > 0)
    back = gather()

    def leave(tau, u):
        return pltpu.make_async_copy(n_ref.at[tau, u], out_ref.at[tau + 2, flip(u, par)], sem.at[tau, u])

    def finish(u):
        for tau in range(2):
            n_ref[tau, u] = jnp.dot(back, y_ref[tau, u], preferred_element_type=F32).astype(BF)
            leave(tau, u).start()

    for u in range(4):
        for tau in range(4):
            frames = [f for f in range(2) if 0 <= f - tau + 2 <= 2]
            acc = taps(s_ref, [(f, u, f - tau + 2, (0, 1, 2)) for f in frames], w2_ref, par) + z_ref[tau, u]
            if tau < 2:
                acc_ref[tau, u] = acc
            else:
                y_ref[tau - 2, u] = acc.astype(BF)
        if u:
            finish(u - 1)
    finish(3)
    for u in range(4):
        for tau in range(2):
            leave(tau, u).wait()


def add_kernel(acc_ref, p_ref, full_ref, out_ref, n_ref, sem):
    par, _ = here()
    back = gather()
    sent = []
    for t in range(2):
        for u in range(4):
            y = (acc_ref[t, u] + unpack(p_ref[t, u]).astype(F32)).astype(BF)
            n_ref[t, u] = jnp.dot(back, y, preferred_element_type=F32).astype(BF)
            copy = pltpu.make_async_copy(n_ref.at[t, u], out_ref.at[t, flip(u, par)], sem.at[t, u])
            copy.start()
            sent.append(copy)
    for copy in sent:
        copy.wait()


VMEM = pl.BlockSpec(memory_space=pltpu.VMEM)
ANY = pl.BlockSpec(memory_space=pl.ANY)


def call(kernel, name, ins, outs, scratch, units, limit=32, in_specs=None, out_specs=None, alias={}):
    return pl.pallas_call(
        kernel,
        in_specs=in_specs or [VMEM] * len(ins),
        out_specs=out_specs or [VMEM] * len(outs),
        out_shape=[jax.ShapeDtypeStruct(s, d) for s, d in outs],
        scratch_shapes=scratch,
        compiler_params=pltpu.CompilerParams(vmem_limit_bytes=limit * MB),
        cost_estimate=pl.CostEstimate(
            flops=int(units * 6e8), bytes_accessed=3_000_000, transcendentals=500_000
        ),
        input_output_aliases=alias,
        name=name,
    )(*ins)


def local(frames_in, gain_one, conv_one, bias_one, gain_two, conv_two, bias_two):
    n = lax.axis_size("rows")
    near = [(i, i ^ 1) for i in range(n)]
    far = [(i, i + 1) for i in range(1, n - 1, 2)] + [(i + 1, i) for i in range(1, n - 1, 2)]
    diag = [(i, n + j) for i, j in far]
    kv = jnp.stack([gain_one, bias_one, gain_two, bias_two])

    own, bs, as_, ts, ds = call(
        prep_kernel, "prep", [frames_in, kv],
        [((4, 4, 3, E, 128), BF), ((4, 2, D, 128), BF), ((4, 2, D, 128), BF), ((2, 4, D, 128), BF), ((2, 2, D, 128), BF)],
        [], 40,
    )
    ar = lax.ppermute(as_, "rows", near)
    br = lax.ppermute(bs, "rows", far)
    ts, ds, ar = lax.optimization_barrier((ts, ds, ar))
    tr = lax.ppermute(ts, "tm", [(0, 1)])
    dr = lax.ppermute(ds, ("tm", "rows"), diag)

    se, oacc, iacc, pe, pf = call(
        early_kernel, "early", [own, ar, conv_one, conv_two, kv],
        [((2, 4, W, C), BF), ((2, 4, W, C), F32), ((4, 2, W, C), F32), ((2, 2, D, 128), BF), ((2, 2, W, C), F32)],
        [pltpu.VMEM((4, 6, 3, E, 128), BF), pltpu.VMEM((2, 5, 3, E, 128), BF)], 18,
    )
    sm, ps = call(
        mid_kernel, "mid", [br, iacc, pe, pf, conv_one, conv_two, kv],
        [((2, 2, W, C), BF), ((2, 4, D, 128), BF)],
        [pltpu.VMEM((4, 2, 3, E, 128), BF), pltpu.VMEM((2, 2, 3, E, 128), BF)], 3,
    )
    pr = lax.ppermute(ps, "tm", [(0, 1)])
    jacc, zacc = call(
        wait_kernel, "wait", [br, iacc, se, sm, conv_one, conv_two, kv, frames_in],
        [((2, 2, W, C), F32), ((4, 4, W, C), F32)],
        [pltpu.VMEM((2, 2, 3, E, 128), BF), pltpu.VMEM((2, 6, 3, E, 128), BF)], 20,
    )
    tr, dr, zacc = lax.optimization_barrier((tr, dr, zacc))
    cr = lax.ppermute(jnp.stack([tr[:, 3], tr[:, 2]], axis=1), "rows", near)
    out, acc = call(
        late_kernel, "late", [tr, dr, cr, oacc, jacc, zacc, conv_one, conv_two, kv],
        [((4, 4, W, C), BF), ((2, 4, W, C), F32)],
        [
            pltpu.VMEM((2, 8, 3, E, 128), BF), pltpu.VMEM((2, 6, 3, E, 128), BF), pltpu.VMEM((2, 4, W, C), BF),
            pltpu.VMEM((2, 4, W, C), BF), pltpu.SemaphoreType.DMA((2, 4)),
        ],
        1, out_specs=[ANY, VMEM],
    )
    (out,) = call(
        add_kernel, "add", [acc, pr, out], [((4, 4, W, C), BF)],
        [pltpu.VMEM((2, 4, W, C), BF), pltpu.SemaphoreType.DMA((2, 4))],
        1, in_specs=[VMEM, VMEM, ANY], out_specs=[ANY], alias={2: 0},
    )
    return out


def solution(mesh):
    in_specs = (P("tm", "rows", "roll", None), P(), P(), P(), P(), P(), P())
    out_specs = P("tm", "rows", "roll", None)
    return jax.shard_map(local, mesh=mesh, in_specs=in_specs, out_specs=out_specs, check_vma=False)
```

```python
import jax
import jax.numpy as jnp
from jax import lax
from jax.experimental import pallas as pl
from jax.experimental.pallas import tpu as pltpu
from jax.sharding import PartitionSpec as P

BF = jnp.bfloat16
F32 = jnp.float32
C = 192
W = 160
S = 16
J = W // S
E = W + 2 * S
D = 240
MB = 2**20


def spread(rows, shift):
    n = lax.broadcasted_iota(jnp.int32, (rows, W), 0)
    c = lax.broadcasted_iota(jnp.int32, (rows, W), 1)
    return jnp.where((n & (S - 1)) * J + (n >> 4) - shift == c, 1.0, 0.0).astype(BF)


def gather():
    c = lax.broadcasted_iota(jnp.int32, (W, W), 0)
    n = lax.broadcasted_iota(jnp.int32, (W, W), 1)
    return jnp.where((n & (S - 1)) * J + (n >> 4) == c, 1.0, 0.0).astype(BF)


def flip(n, par):
    return n + par * (3 - 2 * n)


def act(v, gain):
    power = jnp.mean(v * v, axis=-1, keepdims=True)
    h = v * lax.rsqrt(power + 1e-06) * (gain * 0.5)
    return h + h * jnp.tanh(h)


def pack(v):
    hi = v[:, 128:]
    return jnp.concatenate([v[:, :128], jnp.concatenate([hi[:80], hi[80:]], axis=1)], axis=0)


def unpack(d):
    hi = d[W:]
    return jnp.concatenate([d[:W], jnp.concatenate([hi[:, :64], hi[:, 64:]], axis=0)], axis=1)


def edged(v):
    spot = lax.broadcasted_iota(jnp.int32, (S, C), 0)
    last = pltpu.roll(v[W - S :].astype(F32), 1, 0)
    head = pltpu.roll(v[:S].astype(F32), S - 1, 0)
    last = jnp.where(spot == 0, 0.0, last).astype(BF)
    head = jnp.where(spot == S - 1, 0.0, head).astype(BF)
    return jnp.concatenate([last, v, head], axis=0)


def place(ref, t, v, full, above=True):
    hi = full[:, 128:]
    ref[t, v, 0] = full[:, :128]
    on = jnp.concatenate([hi[S:], jnp.zeros((S, C - 128), BF)], axis=0)
    ref[t, v, 1] = jnp.concatenate([hi, on], axis=1)
    ref[t, v, 2, :, 0:64] = hi
    if above:
        ref[t, v - 1, 2, :, 64:128] = hi


def put(ref, at, v, above=True):
    place(ref, at[0], at[1], edged(v), above)


def taps(src, todo, w, par):
    ins, wts = [], []
    for t, v, a, ps in todo:
        at = {p: p + par * (2 - 2 * p) for p in ps}
        for p in ps:
            for q in range(3):
                ins.append(src[t, v + p, 0, S * q : S * q + W, :])
                wts.append(w[a, at[p], q, 0:128, :])
            ins.append(src[t, v + p, 1, 0:W, :])
            wts.append(jnp.concatenate([w[a, at[p], q, 128:C, :] for q in range(2)], axis=0))
        ps = list(ps)
        while ps:
            p = ps.pop(0)
            if ps:
                more = w[a, at[ps.pop(0)], 2, 128:C, :]
                ins.append(src[t, v + p, 2, 2 * S : E, :])
            else:
                more = jnp.zeros((C - 128, C), BF)
                ins.append(src[t, v + p, 1, 2 * S : E, :])
            wts.append(jnp.concatenate([w[a, at[p], 2, 128:C, :], more], axis=0))
    acc = jnp.zeros((W, C), F32)
    for i in range(0, len(ins), 2):
        left = jnp.concatenate(ins[i : i + 2], axis=1)
        right = jnp.concatenate(wts[i : i + 2], axis=0)
        acc = acc + jnp.dot(left, right, preferred_element_type=F32)
    return acc


def here():
    r = lax.axis_index("rows")
    keep = jnp.where((r == 0) | (r == lax.axis_size("rows") - 1), 0.0, 1.0).astype(F32)
    return r % 2, keep


def has_next():
    return lax.axis_index("tm") < lax.axis_size("tm") - 1


def has_last():
    return lax.axis_index("tm") > 0


def prep_kernel(x_ref, k_ref, own_ref, b_ref, a_ref, t_ref, d_ref):
    par, _ = here()
    m = spread(E, 1)
    g = k_ref[0:1, :]
    for t in range(4):
        for u in range(4):
            xp = jnp.dot(m, x_ref[t, flip(u, par)], preferred_element_type=F32)
            f = act(xp, g).astype(BF)
            own_ref[t, u] = f
            d = pack(f[S : S + W])
            if u < 2:
                b_ref[t, u] = d
                if t >= 2:
                    d_ref[t - 2, u] = d
            else:
                a_ref[t, 3 - u] = d
            if t >= 2:
                t_ref[t - 2, u] = d


def early_kernel(own_ref, a_ref, w1_ref, w2_ref, k_ref, r_ref, o_ref, i_ref, pe_ref, pf_ref, x_ref, s_ref):
    par, _ = here()
    for t in range(4):
        for u in range(4):
            place(x_ref, t, u, own_ref[t, u], above=u > 0)
        for k in range(2):
            put(x_ref, (t, 4 + k), unpack(a_ref[t, k]))
    bias, g = k_ref[1:2, :], k_ref[2:3, :]
    all3 = (0, 1, 2)

    def row(k, _):
        for tau in range(2):
            acc = taps(x_ref, [(tau + a, k, a, all3) for a in range(3)], w1_ref, par)
            f = act(acc + bias, g).astype(BF)
            r_ref[tau, k] = f
            put(s_ref, (tau, k + 1), f)
        o_ref[0, k] = taps(x_ref, [(0, k, 2, all3)], w1_ref, par)
        o_ref[1, k] = taps(x_ref, [(a - 1, k, a, all3) for a in (1, 2)], w1_ref, par)
        return 0

    lax.fori_loop(0, 4, row, 0)
    for tau in range(4):
        ok = [a for a in range(3) if tau + a >= 2]
        i_ref[tau, 0] = taps(x_ref, [(tau + a - 2, -2, a, (2,)) for a in ok], w1_ref, par)
        i_ref[tau, 1] = taps(x_ref, [(tau + a - 2, -1, a, (1, 2)) for a in ok], w1_ref, par)

    @pl.when(has_next())
    def _():
        for tau in range(2):
            ok = range(2 - tau)
            pf_ref[tau, 0] = taps(s_ref, [(tau + a, -1, a, (2,)) for a in ok], w2_ref, par)
            pf_ref[tau, 1] = taps(s_ref, [(tau + a, 0, a, (1, 2)) for a in ok], w2_ref, par)
            for u in range(2):
                acc = taps(s_ref, [(tau + a, u + 1, a, all3) for a in ok], w2_ref, par)
                pe_ref[tau, u] = pack(acc.astype(BF))


def mid_kernel(bx_ref, i_ref, pe_ref, pf_ref, w1_ref, w2_ref, k_ref, r_ref, p_ref, x_ref, s_ref):
    par, keep = here()
    for t in range(4):
        for k in (1, 0):
            put(x_ref, (t, 1 - k), unpack(bx_ref[t, k]), above=k == 0)
    bias, g = k_ref[1:2, :], k_ref[2:3, :]
    for tau in range(2):
        acc = taps(x_ref, [(tau + a, 0, a, (0, 1)) for a in range(3)], w1_ref, par)
        r_ref[tau, 0] = (act(acc + i_ref[tau + 2, 0] + bias, g) * keep).astype(BF)
        acc = taps(x_ref, [(tau + a, 1, a, (0,)) for a in range(3)], w1_ref, par)
        r_ref[tau, 1] = act(acc + i_ref[tau + 2, 1] + bias, g).astype(BF)

    @pl.when(has_next())
    def _():
        for tau in range(2):
            for v in range(2):
                put(s_ref, (tau, v), r_ref[tau, v], above=v > 0)
        for tau in range(2):
            for u in range(2):
                p_ref[tau, u + 2] = pe_ref[tau, u]
            ok = range(2 - tau)
            acc = taps(s_ref, [(tau + a, 0, a, (0, 1)) for a in ok], w2_ref, par)
            p_ref[tau, 0] = pack((acc + pf_ref[tau, 0]).astype(BF))
            acc = taps(s_ref, [(tau + a, 1, a, (0,)) for a in ok], w2_ref, par)
            p_ref[tau, 1] = pack((acc + pf_ref[tau, 1]).astype(BF))


def wait_kernel(bx_ref, i_ref, re_ref, rm_ref, w1_ref, w2_ref, k_ref, in_ref, j_ref, z_ref, x_ref, s_ref):
    par, _ = here()
    for t in range(2):
        for k in (1, 0):
            put(x_ref, (t, 1 - k), unpack(bx_ref[t, k]), above=k == 0)
        for v in range(6):
            put(s_ref, (t, v), rm_ref[t, v] if v < 2 else re_ref[t, v - 2], above=v > 0)
    for tau in range(2):
        ok = [a for a in range(3) if tau + a >= 2]
        acc = taps(x_ref, [(tau + a - 2, 0, a, (0, 1)) for a in ok], w1_ref, par)
        j_ref[tau, 0] = acc + i_ref[tau, 0]
        acc = taps(x_ref, [(tau + a - 2, 1, a, (0,)) for a in ok], w1_ref, par)
        j_ref[tau, 1] = acc + i_ref[tau, 1]
    bias2 = k_ref[3:4, :]
    m = spread(W, 0)

    def row(u, _):
        at = flip(u, par)
        for tau in range(4):
            start = jnp.dot(m, in_ref[tau, at], preferred_element_type=F32) + bias2
            if tau >= 2:
                todo = [(f, u, f - tau + 4, (0, 1, 2)) for f in range(tau - 1)]
                start = start + taps(s_ref, todo, w2_ref, par)
            z_ref[tau, u] = start
        return 0

    lax.fori_loop(0, 4, row, 0)


def recent(x_ref, r_ref, o_ref, k_ref, w1_ref, par, rows, off, fetch, scale):
    bias, g = k_ref[1:2, :], k_ref[2:3, :]

    @pl.when(has_last())
    def _():
        for v in (rows[0] - off, rows[0] - off + 1):
            fetch(v)
        for v in rows:
            fetch(v - off + 2)
            for tau in range(2):
                acc = taps(x_ref, [(tau + a, v - off, a, (0, 1, 2)) for a in range(2 - tau)], w1_ref, par)
                r_ref[tau, v - off] = scale(v, act(acc + o_ref(tau, v) + bias, g)).astype(BF)

    @pl.when(jnp.logical_not(has_last()))
    def _():
        for v in rows:
            for tau in range(2):
                r_ref[tau, v - off] = scale(v, act(o_ref(tau, v) + bias, g)).astype(BF)


def late_kernel(t_ref, d_ref, o_ref, j_ref, w1_ref, k_ref, r_ref, x_ref):
    par, keep = here()

    def fetch(v):
        for t in range(2):
            put(x_ref, (t, v), unpack(d_ref[t, 1 - v] if v < 2 else t_ref[t, v - 2]), above=v > 0)

    recent(
        x_ref, r_ref, lambda tau, v: j_ref[tau, v] if v < 2 else o_ref[tau, v - 2], k_ref, w1_ref, par,
        range(4), 0, fetch, lambda v, f: f if v else f * keep,
    )


def last_kernel(
    t_ref, c_ref, o_ref, r_ref, z_ref, w1_ref, w2_ref, k_ref,
    out_ref, acc_ref, x_ref, s_ref, q_ref, y_ref, n_ref, sem,
):
    par, _ = here()

    def fetch(v):
        for t in range(2):
            put(x_ref, (t, v), unpack(t_ref[t, v + 2] if v < 2 else c_ref[t, v - 2]), above=v > 0)

    recent(
        x_ref, q_ref, lambda tau, v: o_ref[tau, v - 2], k_ref, w1_ref, par,
        range(4, 6), 4, fetch, lambda v, f: f,
    )
    for v in range(6):
        for tau in range(2):
            put(s_ref, (tau, v), r_ref[tau, v] if v < 4 else q_ref[tau, v - 4], above=v > 0)
    back = gather()

    def leave(tau, u):
        return pltpu.make_async_copy(n_ref.at[tau, u], out_ref.at[tau + 2, flip(u, par)], sem.at[tau, u])

    def finish(u):
        for tau in range(2):
            n_ref[tau, u] = jnp.dot(back, y_ref[tau, u], preferred_element_type=F32).astype(BF)
            leave(tau, u).start()

    for u in range(4):
        for tau in (2, 3, 0, 1):
            frames = [f for f in range(2) if 0 <= f - tau + 2 <= 2]
            acc = taps(s_ref, [(f, u, f - tau + 2, (0, 1, 2)) for f in frames], w2_ref, par) + z_ref[tau, u]
            if tau < 2:
                acc_ref[tau, u] = acc
            else:
                y_ref[tau - 2, u] = acc.astype(BF)
        finish(u)
    for u in range(4):
        for tau in range(2):
            leave(tau, u).wait()


def add_kernel(acc_ref, p_ref, full_ref, out_ref, n_ref, sem):
    par, _ = here()
    back = gather()
    sent = []
    for t in range(2):
        for u in range(4):
            y = (acc_ref[t, u] + unpack(p_ref[t, u]).astype(F32)).astype(BF)
            n_ref[t, u] = jnp.dot(back, y, preferred_element_type=F32).astype(BF)
            copy = pltpu.make_async_copy(n_ref.at[t, u], out_ref.at[t, flip(u, par)], sem.at[t, u])
            copy.start()
            sent.append(copy)
    for copy in sent:
        copy.wait()


VMEM = pl.BlockSpec(memory_space=pltpu.VMEM)
ANY = pl.BlockSpec(memory_space=pl.ANY)


def call(kernel, name, ins, outs, scratch, units, limit=32, in_specs=None, out_specs=None, alias={}):
    return pl.pallas_call(
        kernel,
        in_specs=in_specs or [VMEM] * len(ins),
        out_specs=out_specs or [VMEM] * len(outs),
        out_shape=[jax.ShapeDtypeStruct(s, d) for s, d in outs],
        scratch_shapes=scratch,
        compiler_params=pltpu.CompilerParams(vmem_limit_bytes=limit * MB),
        cost_estimate=pl.CostEstimate(
            flops=int(units * 6e8), bytes_accessed=3_000_000, transcendentals=500_000
        ),
        input_output_aliases=alias,
        name=name,
    )(*ins)


def local(frames_in, gain_one, conv_one, bias_one, gain_two, conv_two, bias_two):
    n = lax.axis_size("rows")
    near = [(i, i ^ 1) for i in range(n)]
    far = [(i, i + 1) for i in range(1, n - 1, 2)] + [(i + 1, i) for i in range(1, n - 1, 2)]
    diag = [(i, n + j) for i, j in far]
    kv = jnp.stack([gain_one, bias_one, gain_two, bias_two])

    own, bs, as_, ts, ds = call(
        prep_kernel, "prep", [frames_in, kv],
        [((4, 4, E, C), BF), ((4, 2, D, 128), BF), ((4, 2, D, 128), BF), ((2, 4, D, 128), BF), ((2, 2, D, 128), BF)],
        [], 40,
    )
    ar = lax.ppermute(as_, "rows", near)
    br = lax.ppermute(bs, "rows", far)
    ts, ar = lax.optimization_barrier((ts, ar))
    tr = lax.ppermute(ts, "tm", [(0, 1)])
    se, oacc, iacc, pe, pf = call(
        early_kernel, "early", [own, ar, conv_one, conv_two, kv],
        [((2, 4, W, C), BF), ((2, 4, W, C), F32), ((4, 2, W, C), F32), ((2, 2, D, 128), BF), ((2, 2, W, C), F32)],
        [pltpu.VMEM((4, 6, 3, E, 128), BF), pltpu.VMEM((2, 5, 3, E, 128), BF)], 18,
    )
    ds, pe = lax.optimization_barrier((ds, pe))
    dr = lax.ppermute(ds, ("tm", "rows"), diag)
    sm, ps = call(
        mid_kernel, "mid", [br, iacc, pe, pf, conv_one, conv_two, kv],
        [((2, 2, W, C), BF), ((2, 4, D, 128), BF)],
        [pltpu.VMEM((4, 2, 3, E, 128), BF), pltpu.VMEM((2, 2, 3, E, 128), BF)], 3,
    )
    pr = lax.ppermute(ps, "tm", [(0, 1)])
    jacc, zacc = call(
        wait_kernel, "wait", [br, iacc, se, sm, conv_one, conv_two, kv, frames_in],
        [((2, 2, W, C), F32), ((4, 4, W, C), F32)],
        [pltpu.VMEM((2, 2, 3, E, 128), BF), pltpu.VMEM((2, 6, 3, E, 128), BF)], 20,
    )
    tr, dr, zacc = lax.optimization_barrier((tr, dr, zacc))
    cr = lax.ppermute(jnp.stack([tr[:, 3], tr[:, 2]], axis=1), "rows", near)
    (rs,) = call(
        late_kernel, "late", [tr, dr, oacc, jacc, conv_one, kv], [((2, 4, W, C), BF)],
        [pltpu.VMEM((2, 6, 3, E, 128), BF)], 1,
    )
    rs, cr = lax.optimization_barrier((rs, cr))
    out, acc = call(
        last_kernel, "last", [tr, cr, oacc, rs, zacc, conv_one, conv_two, kv],
        [((4, 4, W, C), BF), ((2, 4, W, C), F32)],
        [
            pltpu.VMEM((2, 4, 3, E, 128), BF), pltpu.VMEM((2, 6, 3, E, 128), BF), pltpu.VMEM((2, 2, W, C), BF),
            pltpu.VMEM((2, 4, W, C), BF), pltpu.VMEM((2, 4, W, C), BF), pltpu.SemaphoreType.DMA((2, 4)),
        ],
        1, out_specs=[ANY, VMEM],
    )
    (out,) = call(
        add_kernel, "add", [acc, pr, out], [((4, 4, W, C), BF)],
        [pltpu.VMEM((2, 4, W, C), BF), pltpu.SemaphoreType.DMA((2, 4))],
        1, in_specs=[VMEM, VMEM, ANY], out_specs=[ANY], alias={2: 0},
    )
    return out


def solution(mesh):
    in_specs = (P("tm", "rows", "roll", None), P(), P(), P(), P(), P(), P())
    out_specs = P("tm", "rows", "roll", None)
    return jax.shard_map(local, mesh=mesh, in_specs=in_specs, out_specs=out_specs, check_vma=False)
```

```python
import jax
import jax.numpy as jnp
from jax import lax
from jax.experimental import pallas as pl
from jax.experimental.pallas import tpu as pltpu
from jax.sharding import PartitionSpec as P

BF = jnp.bfloat16
F32 = jnp.float32
C = 192
W = 160
S = 16
J = W // S
E = W + 2 * S
D = 240
MB = 2**20


def spread(rows, shift):
    n = lax.broadcasted_iota(jnp.int32, (rows, W), 0)
    c = lax.broadcasted_iota(jnp.int32, (rows, W), 1)
    return jnp.where((n & (S - 1)) * J + (n >> 4) - shift == c, 1.0, 0.0).astype(BF)


def gather():
    c = lax.broadcasted_iota(jnp.int32, (W, W), 0)
    n = lax.broadcasted_iota(jnp.int32, (W, W), 1)
    return jnp.where((n & (S - 1)) * J + (n >> 4) == c, 1.0, 0.0).astype(BF)


def flip(n, par):
    return n + par * (3 - 2 * n)


def act(v, gain):
    power = jnp.mean(v * v, axis=-1, keepdims=True)
    h = v * lax.rsqrt(power + 1e-06) * (gain * 0.5)
    return h + h * jnp.tanh(h)


def pack(v):
    hi = v[:, 128:]
    return jnp.concatenate([v[:, :128], jnp.concatenate([hi[:80], hi[80:]], axis=1)], axis=0)


def unpack(d):
    hi = d[W:]
    return jnp.concatenate([d[:W], jnp.concatenate([hi[:, :64], hi[:, 64:]], axis=0)], axis=1)


def edged(v):
    spot = lax.broadcasted_iota(jnp.int32, (S, C), 0)
    last = pltpu.roll(v[W - S :].astype(F32), 1, 0)
    head = pltpu.roll(v[:S].astype(F32), S - 1, 0)
    last = jnp.where(spot == 0, 0.0, last).astype(BF)
    head = jnp.where(spot == S - 1, 0.0, head).astype(BF)
    return jnp.concatenate([last, v, head], axis=0)


def place(ref, t, v, full, above=True):
    hi = full[:, 128:]
    ref[t, v, 0] = full[:, :128]
    on = jnp.concatenate([hi[S:], jnp.zeros((S, C - 128), BF)], axis=0)
    ref[t, v, 1] = jnp.concatenate([hi, on], axis=1)
    ref[t, v, 2, :, 0:64] = hi
    if above:
        ref[t, v - 1, 2, :, 64:128] = hi


def put(ref, at, v, above=True):
    place(ref, at[0], at[1], edged(v), above)


def taps(src, todo, w, par):
    ins, wts = [], []
    for t, v, a, ps in todo:
        at = {p: p + par * (2 - 2 * p) for p in ps}
        for p in ps:
            for q in range(3):
                ins.append(src[t, v + p, 0, S * q : S * q + W, :])
                wts.append(w[a, at[p], q, 0:128, :])
            ins.append(src[t, v + p, 1, 0:W, :])
            wts.append(jnp.concatenate([w[a, at[p], q, 128:C, :] for q in range(2)], axis=0))
        ps = list(ps)
        while ps:
            p = ps.pop(0)
            if ps:
                more = w[a, at[ps.pop(0)], 2, 128:C, :]
                ins.append(src[t, v + p, 2, 2 * S : E, :])
            else:
                more = jnp.zeros((C - 128, C), BF)
                ins.append(src[t, v + p, 1, 2 * S : E, :])
            wts.append(jnp.concatenate([w[a, at[p], 2, 128:C, :], more], axis=0))
    acc = jnp.zeros((W, C), F32)
    for i in range(0, len(ins), 2):
        left = jnp.concatenate(ins[i : i + 2], axis=1)
        right = jnp.concatenate(wts[i : i + 2], axis=0)
        acc = acc + jnp.dot(left, right, preferred_element_type=F32)
    return acc


def here():
    r = lax.axis_index("rows")
    keep = jnp.where((r == 0) | (r == lax.axis_size("rows") - 1), 0.0, 1.0).astype(F32)
    return r % 2, keep


def has_next():
    return lax.axis_index("tm") < lax.axis_size("tm") - 1


def has_last():
    return lax.axis_index("tm") > 0


def prep_kernel(x_ref, k_ref, own_ref, b_ref, a_ref, t_ref, d_ref):
    par, _ = here()
    m = spread(E, 1)
    g = k_ref[0:1, :]
    for t in range(4):
        for u in range(4):
            xp = jnp.dot(m, x_ref[t, flip(u, par)], preferred_element_type=F32)
            f = act(xp, g).astype(BF)
            own_ref[t, u] = f
            d = pack(f[S : S + W])
            if u < 2:
                b_ref[t, u] = d
                if t >= 2:
                    d_ref[t - 2, u] = d
            else:
                a_ref[t, 3 - u] = d
            if t >= 2:
                t_ref[t - 2, u] = d


def early_kernel(own_ref, a_ref, w1_ref, w2_ref, k_ref, r_ref, o_ref, i_ref, pe_ref, pf_ref, x_ref, s_ref):
    par, _ = here()
    for t in range(4):
        for u in range(4):
            place(x_ref, t, u, own_ref[t, u], above=u > 0)
        for k in range(2):
            put(x_ref, (t, 4 + k), unpack(a_ref[t, k]))
    bias, g = k_ref[1:2, :], k_ref[2:3, :]
    all3 = (0, 1, 2)

    def row(k, _):
        for tau in range(2):
            acc = taps(x_ref, [(tau + a, k, a, all3) for a in range(3)], w1_ref, par)
            f = act(acc + bias, g).astype(BF)
            r_ref[tau, k] = f
            put(s_ref, (tau, k + 1), f)
        o_ref[0, k] = taps(x_ref, [(0, k, 2, all3)], w1_ref, par)
        o_ref[1, k] = taps(x_ref, [(a - 1, k, a, all3) for a in (1, 2)], w1_ref, par)
        return 0

    lax.fori_loop(0, 4, row, 0)
    for tau in range(4):
        ok = [a for a in range(3) if tau + a >= 2]
        i_ref[tau, 0] = taps(x_ref, [(tau + a - 2, -2, a, (2,)) for a in ok], w1_ref, par)
        i_ref[tau, 1] = taps(x_ref, [(tau + a - 2, -1, a, (1, 2)) for a in ok], w1_ref, par)

    @pl.when(has_next())
    def _():
        for tau in range(2):
            ok = range(2 - tau)
            pf_ref[tau, 0] = taps(s_ref, [(tau + a, -1, a, (2,)) for a in ok], w2_ref, par)
            pf_ref[tau, 1] = taps(s_ref, [(tau + a, 0, a, (1, 2)) for a in ok], w2_ref, par)
            for u in range(2):
                acc = taps(s_ref, [(tau + a, u + 1, a, all3) for a in ok], w2_ref, par)
                pe_ref[tau, u] = pack(acc.astype(BF))


def mid_kernel(bx_ref, i_ref, pe_ref, pf_ref, w1_ref, w2_ref, k_ref, r_ref, p_ref, x_ref, s_ref):
    par, keep = here()
    for t in range(4):
        for k in (1, 0):
            put(x_ref, (t, 1 - k), unpack(bx_ref[t, k]), above=k == 0)
    bias, g = k_ref[1:2, :], k_ref[2:3, :]
    for tau in range(2):
        acc = taps(x_ref, [(tau + a, 0, a, (0, 1)) for a in range(3)], w1_ref, par)
        r_ref[tau, 0] = (act(acc + i_ref[tau + 2, 0] + bias, g) * keep).astype(BF)
        acc = taps(x_ref, [(tau + a, 1, a, (0,)) for a in range(3)], w1_ref, par)
        r_ref[tau, 1] = act(acc + i_ref[tau + 2, 1] + bias, g).astype(BF)

    @pl.when(has_next())
    def _():
        for tau in range(2):
            for v in range(2):
                put(s_ref, (tau, v), r_ref[tau, v], above=v > 0)
        for tau in range(2):
            for u in range(2):
                p_ref[tau, u + 2] = pe_ref[tau, u]
            ok = range(2 - tau)
            acc = taps(s_ref, [(tau + a, 0, a, (0, 1)) for a in ok], w2_ref, par)
            p_ref[tau, 0] = pack((acc + pf_ref[tau, 0]).astype(BF))
            acc = taps(s_ref, [(tau + a, 1, a, (0,)) for a in ok], w2_ref, par)
            p_ref[tau, 1] = pack((acc + pf_ref[tau, 1]).astype(BF))


def wait_kernel(bx_ref, i_ref, re_ref, rm_ref, w1_ref, w2_ref, k_ref, in_ref, j_ref, z_ref, x_ref, s_ref):
    par, _ = here()
    for t in range(2):
        for k in (1, 0):
            put(x_ref, (t, 1 - k), unpack(bx_ref[t, k]), above=k == 0)
        for v in range(6):
            put(s_ref, (t, v), rm_ref[t, v] if v < 2 else re_ref[t, v - 2], above=v > 0)
    for tau in range(2):
        ok = [a for a in range(3) if tau + a >= 2]
        acc = taps(x_ref, [(tau + a - 2, 0, a, (0, 1)) for a in ok], w1_ref, par)
        j_ref[tau, 0] = acc + i_ref[tau, 0]
        acc = taps(x_ref, [(tau + a - 2, 1, a, (0,)) for a in ok], w1_ref, par)
        j_ref[tau, 1] = acc + i_ref[tau, 1]
    bias2 = k_ref[3:4, :]
    m = spread(W, 0)

    def row(u, _):
        at = flip(u, par)
        for tau in range(4):
            start = jnp.dot(m, in_ref[tau, at], preferred_element_type=F32) + bias2
            if tau >= 2:
                todo = [(f, u, f - tau + 4, (0, 1, 2)) for f in range(tau - 1)]
                start = start + taps(s_ref, todo, w2_ref, par)
            z_ref[tau, u] = start
        return 0

    lax.fori_loop(0, 4, row, 0)


def recent(x_ref, r_ref, o_ref, k_ref, w1_ref, par, rows, off, fetch, scale, also):
    bias, g = k_ref[1:2, :], k_ref[2:3, :]

    @pl.when(has_last())
    def _():
        for v in (rows[0] - off, rows[0] - off + 1):
            fetch(v)
        for v in rows:
            fetch(v - off + 2)
            also(v)
            for tau in range(2):
                acc = taps(x_ref, [(tau + a, v - off, a, (0, 1, 2)) for a in range(2 - tau)], w1_ref, par)
                r_ref[tau, v - off] = scale(v, act(acc + o_ref(tau, v) + bias, g)).astype(BF)

    @pl.when(jnp.logical_not(has_last()))
    def _():
        for v in rows:
            also(v)
            for tau in range(2):
                r_ref[tau, v - off] = scale(v, act(o_ref(tau, v) + bias, g)).astype(BF)


def late_kernel(t_ref, d_ref, o_ref, j_ref, w1_ref, k_ref, r_ref, x_ref):
    par, keep = here()

    def fetch(v):
        for t in range(2):
            put(x_ref, (t, v), unpack(d_ref[t, 1 - v] if v < 2 else t_ref[t, v - 2]), above=v > 0)

    recent(
        x_ref, r_ref, lambda tau, v: j_ref[tau, v] if v < 2 else o_ref[tau, v - 2], k_ref, w1_ref, par,
        range(4), 0, fetch, lambda v, f: f if v else f * keep, lambda v: None,
    )


def last_kernel(
    t_ref, c_ref, o_ref, r_ref, z_ref, w1_ref, w2_ref, k_ref,
    out_ref, acc_ref, x_ref, s_ref, q_ref, y_ref, n_ref, sem,
):
    par, _ = here()

    def fetch(v):
        for t in range(2):
            put(x_ref, (t, v), unpack(t_ref[t, v + 2] if v < 2 else c_ref[t, v - 2]), above=v > 0)

    def ready(v):
        for n in (2 * v - 8, 2 * v - 7):
            for tau in range(2):
                put(s_ref, (tau, n), r_ref[tau, n], above=n > 0)

    recent(
        x_ref, q_ref, lambda tau, v: o_ref[tau, v - 2], k_ref, w1_ref, par,
        range(4, 6), 4, fetch, lambda v, f: f, ready,
    )
    for tau in range(2):
        for v in (4, 5):
            put(s_ref, (tau, v), q_ref[tau, v - 4])
    back = gather()

    def leave(tau, u):
        return pltpu.make_async_copy(n_ref.at[tau, u], out_ref.at[tau + 2, flip(u, par)], sem.at[tau, u])

    def finish(u):
        for tau in range(2):
            n_ref[tau, u] = jnp.dot(back, y_ref[tau, u], preferred_element_type=F32).astype(BF)
            leave(tau, u).start()

    for u in range(4):
        for tau in (2, 3, 0, 1):
            frames = [f for f in range(2) if 0 <= f - tau + 2 <= 2]
            acc = taps(s_ref, [(f, u, f - tau + 2, (0, 1, 2)) for f in frames], w2_ref, par) + z_ref[tau, u]
            if tau < 2:
                acc_ref[tau, u] = acc
            else:
                y_ref[tau - 2, u] = acc.astype(BF)
        finish(u)
    for u in range(4):
        for tau in range(2):
            leave(tau, u).wait()


def add_kernel(acc_ref, p_ref, full_ref, out_ref, n_ref, sem):
    par, _ = here()
    back = gather()
    sent = []
    for t in range(2):
        for u in range(4):
            y = (acc_ref[t, u] + unpack(p_ref[t, u]).astype(F32)).astype(BF)
            n_ref[t, u] = jnp.dot(back, y, preferred_element_type=F32).astype(BF)
            copy = pltpu.make_async_copy(n_ref.at[t, u], out_ref.at[t, flip(u, par)], sem.at[t, u])
            copy.start()
            sent.append(copy)
    for copy in sent:
        copy.wait()


VMEM = pl.BlockSpec(memory_space=pltpu.VMEM)
ANY = pl.BlockSpec(memory_space=pl.ANY)


def call(kernel, name, ins, outs, scratch, units, limit=32, in_specs=None, out_specs=None, alias={}):
    return pl.pallas_call(
        kernel,
        in_specs=in_specs or [VMEM] * len(ins),
        out_specs=out_specs or [VMEM] * len(outs),
        out_shape=[jax.ShapeDtypeStruct(s, d) for s, d in outs],
        scratch_shapes=scratch,
        compiler_params=pltpu.CompilerParams(vmem_limit_bytes=limit * MB),
        cost_estimate=pl.CostEstimate(
            flops=int(units * 6e8), bytes_accessed=3_000_000, transcendentals=500_000
        ),
        input_output_aliases=alias,
        name=name,
    )(*ins)


def local(frames_in, gain_one, conv_one, bias_one, gain_two, conv_two, bias_two):
    n = lax.axis_size("rows")
    near = [(i, i ^ 1) for i in range(n)]
    far = [(i, i + 1) for i in range(1, n - 1, 2)] + [(i + 1, i) for i in range(1, n - 1, 2)]
    diag = [(i, n + j) for i, j in far]
    kv = jnp.stack([gain_one, bias_one, gain_two, bias_two])

    own, bs, as_, ts, ds = call(
        prep_kernel, "prep", [frames_in, kv],
        [((4, 4, E, C), BF), ((4, 2, D, 128), BF), ((4, 2, D, 128), BF), ((2, 4, D, 128), BF), ((2, 2, D, 128), BF)],
        [], 40,
    )
    ar = lax.ppermute(as_, "rows", near)
    br = lax.ppermute(bs, "rows", far)
    ts, ds, ar = lax.optimization_barrier((ts, ds, ar))
    tr = lax.ppermute(ts, "tm", [(0, 1)])
    se, oacc, iacc, pe, pf = call(
        early_kernel, "early", [own, ar, conv_one, conv_two, kv],
        [((2, 4, W, C), BF), ((2, 4, W, C), F32), ((4, 2, W, C), F32), ((2, 2, D, 128), BF), ((2, 2, W, C), F32)],
        [pltpu.VMEM((4, 6, 3, E, 128), BF), pltpu.VMEM((2, 5, 3, E, 128), BF)], 18,
    )
    dr = lax.ppermute(ds, ("tm", "rows"), diag)
    sm, ps = call(
        mid_kernel, "mid", [br, iacc, pe, pf, conv_one, conv_two, kv],
        [((2, 2, W, C), BF), ((2, 4, D, 128), BF)],
        [pltpu.VMEM((4, 2, 3, E, 128), BF), pltpu.VMEM((2, 2, 3, E, 128), BF)], 3,
    )
    pr = lax.ppermute(ps, "tm", [(0, 1)])
    jacc, zacc = call(
        wait_kernel, "wait", [br, iacc, se, sm, conv_one, conv_two, kv, frames_in],
        [((2, 2, W, C), F32), ((4, 4, W, C), F32)],
        [pltpu.VMEM((2, 2, 3, E, 128), BF), pltpu.VMEM((2, 6, 3, E, 128), BF)], 20,
    )
    tr, zacc = lax.optimization_barrier((tr, zacc))
    cr = lax.ppermute(jnp.stack([tr[:, 3], tr[:, 2]], axis=1), "rows", near)
    (rs,) = call(
        late_kernel, "late", [tr, dr, oacc, jacc, conv_one, kv], [((2, 4, W, C), BF)],
        [pltpu.VMEM((2, 6, 3, E, 128), BF)], 1,
    )
    rs, cr = lax.optimization_barrier((rs, cr))
    out, acc = call(
        last_kernel, "last", [tr, cr, oacc, rs, zacc, conv_one, conv_two, kv],
        [((4, 4, W, C), BF), ((2, 4, W, C), F32)],
        [
            pltpu.VMEM((2, 4, 3, E, 128), BF), pltpu.VMEM((2, 6, 3, E, 128), BF), pltpu.VMEM((2, 2, W, C), BF),
            pltpu.VMEM((2, 4, W, C), BF), pltpu.VMEM((2, 4, W, C), BF), pltpu.SemaphoreType.DMA((2, 4)),
        ],
        1, out_specs=[ANY, VMEM],
    )
    (out,) = call(
        add_kernel, "add", [acc, pr, out], [((4, 4, W, C), BF)],
        [pltpu.VMEM((2, 4, W, C), BF), pltpu.SemaphoreType.DMA((2, 4))],
        1, in_specs=[VMEM, VMEM, ANY], out_specs=[ANY], alias={2: 0},
    )
    return out


def solution(mesh):
    in_specs = (P("tm", "rows", "roll", None), P(), P(), P(), P(), P(), P())
    out_specs = P("tm", "rows", "roll", None)
    return jax.shard_map(local, mesh=mesh, in_specs=in_specs, out_specs=out_specs, check_vma=False)
```

```python
import jax
import jax.numpy as jnp
from jax import lax
from jax.experimental import pallas as pl
from jax.experimental.pallas import tpu as pltpu
from jax.sharding import PartitionSpec as P

BF = jnp.bfloat16
F32 = jnp.float32
C = 192
W = 160
S = 16
J = W // S
E = W + 2 * S
D = 240
MB = 2**20


def spread(rows, shift):
    n = lax.broadcasted_iota(jnp.int32, (rows, W), 0)
    c = lax.broadcasted_iota(jnp.int32, (rows, W), 1)
    return jnp.where((n & (S - 1)) * J + (n >> 4) - shift == c, 1.0, 0.0).astype(BF)


def gather():
    c = lax.broadcasted_iota(jnp.int32, (W, W), 0)
    n = lax.broadcasted_iota(jnp.int32, (W, W), 1)
    return jnp.where((n & (S - 1)) * J + (n >> 4) == c, 1.0, 0.0).astype(BF)


def flip(n, par):
    return n + par * (3 - 2 * n)


def act(v, gain):
    power = jnp.mean(v * v, axis=-1, keepdims=True)
    h = v * lax.rsqrt(power + 1e-06) * (gain * 0.5)
    return h + h * jnp.tanh(h)


def pack(v):
    hi = v[:, 128:]
    return jnp.concatenate([v[:, :128], jnp.concatenate([hi[:80], hi[80:]], axis=1)], axis=0)


def unpack(d):
    hi = d[W:]
    return jnp.concatenate([d[:W], jnp.concatenate([hi[:, :64], hi[:, 64:]], axis=0)], axis=1)


def edged(v):
    spot = lax.broadcasted_iota(jnp.int32, (S, C), 0)
    last = pltpu.roll(v[W - S :].astype(F32), 1, 0)
    head = pltpu.roll(v[:S].astype(F32), S - 1, 0)
    last = jnp.where(spot == 0, 0.0, last).astype(BF)
    head = jnp.where(spot == S - 1, 0.0, head).astype(BF)
    return jnp.concatenate([last, v, head], axis=0)


def place(ref, t, v, full, above=True):
    hi = full[:, 128:]
    ref[t, v, 0] = full[:, :128]
    on = jnp.concatenate([hi[S:], jnp.zeros((S, C - 128), BF)], axis=0)
    ref[t, v, 1] = jnp.concatenate([hi, on], axis=1)
    ref[t, v, 2, :, 0:64] = hi
    if above:
        ref[t, v - 1, 2, :, 64:128] = hi


def put(ref, at, v, above=True):
    place(ref, at[0], at[1], edged(v), above)


def taps(src, todo, w, par):
    ins, wts = [], []
    for t, v, a, ps in todo:
        at = {p: p + par * (2 - 2 * p) for p in ps}
        for p in ps:
            for q in range(3):
                ins.append(src[t, v + p, 0, S * q : S * q + W, :])
                wts.append(w[a, at[p], q, 0:128, :])
            ins.append(src[t, v + p, 1, 0:W, :])
            wts.append(jnp.concatenate([w[a, at[p], q, 128:C, :] for q in range(2)], axis=0))
        ps = list(ps)
        while ps:
            p = ps.pop(0)
            if ps:
                more = w[a, at[ps.pop(0)], 2, 128:C, :]
                ins.append(src[t, v + p, 2, 2 * S : E, :])
            else:
                more = jnp.zeros((C - 128, C), BF)
                ins.append(src[t, v + p, 1, 2 * S : E, :])
            wts.append(jnp.concatenate([w[a, at[p], 2, 128:C, :], more], axis=0))
    acc = jnp.zeros((W, C), F32)
    for i in range(0, len(ins), 2):
        left = jnp.concatenate(ins[i : i + 2], axis=1)
        right = jnp.concatenate(wts[i : i + 2], axis=0)
        acc = acc + jnp.dot(left, right, preferred_element_type=F32)
    return acc


def here():
    r = lax.axis_index("rows")
    keep = jnp.where((r == 0) | (r == lax.axis_size("rows") - 1), 0.0, 1.0).astype(F32)
    return r % 2, keep


def has_next():
    return lax.axis_index("tm") < lax.axis_size("tm") - 1


def has_last():
    return lax.axis_index("tm") > 0


def prep_kernel(x_ref, k_ref, own_ref, b_ref, a_ref, t_ref, d_ref):
    par, _ = here()
    m = spread(E, 1)
    g = k_ref[0:1, :]
    for t in range(4):
        for u in range(4):
            xp = jnp.dot(m, x_ref[t, flip(u, par)], preferred_element_type=F32)
            f = act(xp, g).astype(BF)
            own_ref[t, u] = f
            d = pack(f[S : S + W])
            if u < 2:
                b_ref[t, u] = d
                if t >= 2:
                    d_ref[t - 2, u] = d
            else:
                a_ref[t, 3 - u] = d
            if t >= 2:
                t_ref[t - 2, u] = d


def early_kernel(own_ref, a_ref, w1_ref, w2_ref, k_ref, r_ref, o_ref, i_ref, pe_ref, pf_ref, x_ref, s_ref):
    par, _ = here()
    for t in range(4):
        for u in range(4):
            place(x_ref, t, u, own_ref[t, u], above=u > 0)
        for k in range(2):
            put(x_ref, (t, 4 + k), unpack(a_ref[t, k]))
    bias, g = k_ref[1:2, :], k_ref[2:3, :]
    all3 = (0, 1, 2)

    def row(k, _):
        for tau in range(2):
            acc = taps(x_ref, [(tau + a, k, a, all3) for a in range(3)], w1_ref, par)
            f = act(acc + bias, g).astype(BF)
            r_ref[tau, k] = f
            put(s_ref, (tau, k + 1), f)
        o_ref[0, k] = taps(x_ref, [(0, k, 2, all3)], w1_ref, par)
        o_ref[1, k] = taps(x_ref, [(a - 1, k, a, all3) for a in (1, 2)], w1_ref, par)
        return 0

    lax.fori_loop(0, 4, row, 0)
    for tau in range(4):
        ok = [a for a in range(3) if tau + a >= 2]
        i_ref[tau, 0] = taps(x_ref, [(tau + a - 2, -2, a, (2,)) for a in ok], w1_ref, par)
        i_ref[tau, 1] = taps(x_ref, [(tau + a - 2, -1, a, (1, 2)) for a in ok], w1_ref, par)

    @pl.when(has_next())
    def _():
        for tau in range(2):
            ok = range(2 - tau)
            pf_ref[tau, 0] = taps(s_ref, [(tau + a, -1, a, (2,)) for a in ok], w2_ref, par)
            pf_ref[tau, 1] = taps(s_ref, [(tau + a, 0, a, (1, 2)) for a in ok], w2_ref, par)
            for u in range(2):
                acc = taps(s_ref, [(tau + a, u + 1, a, all3) for a in ok], w2_ref, par)
                pe_ref[tau, u] = pack(acc.astype(BF))


def mid_kernel(bx_ref, i_ref, pe_ref, pf_ref, w1_ref, w2_ref, k_ref, r_ref, p_ref, x_ref, s_ref):
    par, keep = here()
    for t in range(4):
        for k in (1, 0):
            put(x_ref, (t, 1 - k), unpack(bx_ref[t, k]), above=k == 0)
    bias, g = k_ref[1:2, :], k_ref[2:3, :]
    for tau in range(2):
        acc = taps(x_ref, [(tau + a, 0, a, (0, 1)) for a in range(3)], w1_ref, par)
        r_ref[tau, 0] = (act(acc + i_ref[tau + 2, 0] + bias, g) * keep).astype(BF)
        acc = taps(x_ref, [(tau + a, 1, a, (0,)) for a in range(3)], w1_ref, par)
        r_ref[tau, 1] = act(acc + i_ref[tau + 2, 1] + bias, g).astype(BF)

    @pl.when(has_next())
    def _():
        for tau in range(2):
            for v in range(2):
                put(s_ref, (tau, v), r_ref[tau, v], above=v > 0)
        for tau in range(2):
            for u in range(2):
                p_ref[tau, u + 2] = pe_ref[tau, u]
            ok = range(2 - tau)
            acc = taps(s_ref, [(tau + a, 0, a, (0, 1)) for a in ok], w2_ref, par)
            p_ref[tau, 0] = pack((acc + pf_ref[tau, 0]).astype(BF))
            acc = taps(s_ref, [(tau + a, 1, a, (0,)) for a in ok], w2_ref, par)
            p_ref[tau, 1] = pack((acc + pf_ref[tau, 1]).astype(BF))


def wait_kernel(bx_ref, i_ref, re_ref, rm_ref, w1_ref, w2_ref, k_ref, in_ref, j_ref, z_ref, x_ref, s_ref):
    par, _ = here()
    for t in range(2):
        for k in (1, 0):
            put(x_ref, (t, 1 - k), unpack(bx_ref[t, k]), above=k == 0)
        for v in range(6):
            put(s_ref, (t, v), rm_ref[t, v] if v < 2 else re_ref[t, v - 2], above=v > 0)
    for tau in range(2):
        ok = [a for a in range(3) if tau + a >= 2]
        acc = taps(x_ref, [(tau + a - 2, 0, a, (0, 1)) for a in ok], w1_ref, par)
        j_ref[tau, 0] = acc + i_ref[tau, 0]
        acc = taps(x_ref, [(tau + a - 2, 1, a, (0,)) for a in ok], w1_ref, par)
        j_ref[tau, 1] = acc + i_ref[tau, 1]
    bias2 = k_ref[3:4, :]
    m = spread(W, 0)

    def row(u, _):
        at = flip(u, par)
        for tau in range(4):
            start = jnp.dot(m, in_ref[tau, at], preferred_element_type=F32) + bias2
            if tau >= 2:
                todo = [(f, u, f - tau + 4, (0, 1, 2)) for f in range(tau - 1)]
                start = start + taps(s_ref, todo, w2_ref, par)
            z_ref[tau, u] = start
        return 0

    lax.fori_loop(0, 4, row, 0)


def recent(x_ref, r_ref, o_ref, k_ref, w1_ref, par, rows, off, fetch, scale, also):
    bias, g = k_ref[1:2, :], k_ref[2:3, :]

    @pl.when(has_last())
    def _():
        for v in (rows[0] - off, rows[0] - off + 1):
            fetch(v)
        for v in rows:
            fetch(v - off + 2)
            also(v)
            for tau in range(2):
                acc = taps(x_ref, [(tau + a, v - off, a, (0, 1, 2)) for a in range(2 - tau)], w1_ref, par)
                r_ref[tau, v - off] = scale(v, act(acc + o_ref(tau, v) + bias, g)).astype(BF)

    @pl.when(jnp.logical_not(has_last()))
    def _():
        for v in rows:
            also(v)
            for tau in range(2):
                r_ref[tau, v - off] = scale(v, act(o_ref(tau, v) + bias, g)).astype(BF)


def late_kernel(t_ref, d_ref, o_ref, j_ref, w1_ref, k_ref, r_ref, x_ref):
    par, keep = here()

    def fetch(v):
        for t in range(2):
            put(x_ref, (t, v), unpack(d_ref[t, 1 - v] if v < 2 else t_ref[t, v - 2]), above=v > 0)

    recent(
        x_ref, r_ref, lambda tau, v: j_ref[tau, v] if v < 2 else o_ref[tau, v - 2], k_ref, w1_ref, par,
        range(4), 0, fetch, lambda v, f: f if v else f * keep, lambda v: None,
    )


def last_kernel(
    t_ref, c_ref, o_ref, r_ref, z_ref, w1_ref, w2_ref, k_ref,
    out_ref, acc_ref, x_ref, s_ref, q_ref, y_ref, n_ref, sem,
):
    par, _ = here()

    def fetch(v):
        for t in range(2):
            put(x_ref, (t, v), unpack(t_ref[t, v + 2] if v < 2 else c_ref[t, v - 2]), above=v > 0)

    def ready(v):
        for n in (2 * v - 8, 2 * v - 7):
            for tau in range(2):
                put(s_ref, (tau, n), r_ref[tau, n], above=n > 0)

    recent(
        x_ref, q_ref, lambda tau, v: o_ref[tau, v - 2], k_ref, w1_ref, par,
        range(4, 6), 4, fetch, lambda v, f: f, ready,
    )
    for tau in range(2):
        for v in (4, 5):
            put(s_ref, (tau, v), q_ref[tau, v - 4])
    back = gather()

    def leave(tau, u):
        return pltpu.make_async_copy(n_ref.at[tau, u], out_ref.at[tau + 2, flip(u, par)], sem.at[tau, u])

    def finish(u):
        for tau in range(2):
            n_ref[tau, u] = jnp.dot(back, y_ref[tau, u], preferred_element_type=F32).astype(BF)
            leave(tau, u).start()

    for u in range(4):
        for tau in (2, 3, 0, 1):
            frames = [f for f in range(2) if 0 <= f - tau + 2 <= 2]
            acc = taps(s_ref, [(f, u, f - tau + 2, (0, 1, 2)) for f in frames], w2_ref, par) + z_ref[tau, u]
            if tau < 2:
                acc_ref[tau, u] = acc
            else:
                y_ref[tau - 2, u] = acc.astype(BF)
        finish(u)
    for u in range(4):
        for tau in range(2):
            leave(tau, u).wait()


def add_kernel(acc_ref, p_ref, full_ref, out_ref, n_ref, sem):
    par, _ = here()
    back = gather()
    sent = []
    for t in range(2):
        for u in range(4):
            y = (acc_ref[t, u] + unpack(p_ref[t, u]).astype(F32)).astype(BF)
            n_ref[t, u] = jnp.dot(back, y, preferred_element_type=F32).astype(BF)
            copy = pltpu.make_async_copy(n_ref.at[t, u], out_ref.at[t, flip(u, par)], sem.at[t, u])
            copy.start()
            sent.append(copy)
    for copy in sent:
        copy.wait()


VMEM = pl.BlockSpec(memory_space=pltpu.VMEM)
ANY = pl.BlockSpec(memory_space=pl.ANY)


def call(kernel, name, ins, outs, scratch, units, limit=32, in_specs=None, out_specs=None, alias={}):
    return pl.pallas_call(
        kernel,
        in_specs=in_specs or [VMEM] * len(ins),
        out_specs=out_specs or [VMEM] * len(outs),
        out_shape=[jax.ShapeDtypeStruct(s, d) for s, d in outs],
        scratch_shapes=scratch,
        compiler_params=pltpu.CompilerParams(vmem_limit_bytes=limit * MB),
        cost_estimate=pl.CostEstimate(
            flops=int(units * 6e8), bytes_accessed=3_000_000, transcendentals=500_000
        ),
        input_output_aliases=alias,
        name=name,
    )(*ins)


def local(frames_in, gain_one, conv_one, bias_one, gain_two, conv_two, bias_two):
    n = lax.axis_size("rows")
    near = [(i, i ^ 1) for i in range(n)]
    far = [(i, i + 1) for i in range(1, n - 1, 2)] + [(i + 1, i) for i in range(1, n - 1, 2)]
    diag = [(i, n + j) for i, j in far]
    kv = jnp.stack([gain_one, bias_one, gain_two, bias_two])

    own, bs, as_, ts, ds = call(
        prep_kernel, "prep", [frames_in, kv],
        [((4, 4, E, C), BF), ((4, 2, D, 128), BF), ((4, 2, D, 128), BF), ((2, 4, D, 128), BF), ((2, 2, D, 128), BF)],
        [], 40,
    )
    ar = lax.ppermute(as_, "rows", near)
    br = lax.ppermute(bs, "rows", far)
    ts, ar = lax.optimization_barrier((ts, ar))
    tr = lax.ppermute(ts, "tm", [(0, 1)])
    se, oacc, iacc, pe, pf = call(
        early_kernel, "early", [own, ar, conv_one, conv_two, kv],
        [((2, 4, W, C), BF), ((2, 4, W, C), F32), ((4, 2, W, C), F32), ((2, 2, D, 128), BF), ((2, 2, W, C), F32)],
        [pltpu.VMEM((4, 6, 3, E, 128), BF), pltpu.VMEM((2, 5, 3, E, 128), BF)], 18,
    )
    kv, ar = lax.optimization_barrier((kv + 0.0 * ar[0, 0, 0, 0].astype(F32), ar))
    ds, kv = lax.optimization_barrier((ds, kv))
    dr = lax.ppermute(ds, ("tm", "rows"), diag)
    sm, ps = call(
        mid_kernel, "mid", [br, iacc, pe, pf, conv_one, conv_two, kv],
        [((2, 2, W, C), BF), ((2, 4, D, 128), BF)],
        [pltpu.VMEM((4, 2, 3, E, 128), BF), pltpu.VMEM((2, 2, 3, E, 128), BF)], 3,
    )
    pr = lax.ppermute(ps, "tm", [(0, 1)])
    jacc, zacc = call(
        wait_kernel, "wait", [br, iacc, se, sm, conv_one, conv_two, kv, frames_in],
        [((2, 2, W, C), F32), ((4, 4, W, C), F32)],
        [pltpu.VMEM((2, 2, 3, E, 128), BF), pltpu.VMEM((2, 6, 3, E, 128), BF)], 20,
    )
    tr, zacc = lax.optimization_barrier((tr, zacc))
    cr = lax.ppermute(jnp.stack([tr[:, 3], tr[:, 2]], axis=1), "rows", near)
    (rs,) = call(
        late_kernel, "late", [tr, dr, oacc, jacc, conv_one, kv], [((2, 4, W, C), BF)],
        [pltpu.VMEM((2, 6, 3, E, 128), BF)], 1,
    )
    rs, cr = lax.optimization_barrier((rs, cr))
    out, acc = call(
        last_kernel, "last", [tr, cr, oacc, rs, zacc, conv_one, conv_two, kv],
        [((4, 4, W, C), BF), ((2, 4, W, C), F32)],
        [
            pltpu.VMEM((2, 4, 3, E, 128), BF), pltpu.VMEM((2, 6, 3, E, 128), BF), pltpu.VMEM((2, 2, W, C), BF),
            pltpu.VMEM((2, 4, W, C), BF), pltpu.VMEM((2, 4, W, C), BF), pltpu.SemaphoreType.DMA((2, 4)),
        ],
        1, out_specs=[ANY, VMEM],
    )
    (out,) = call(
        add_kernel, "add", [acc, pr, out], [((4, 4, W, C), BF)],
        [pltpu.VMEM((2, 4, W, C), BF), pltpu.SemaphoreType.DMA((2, 4))],
        1, in_specs=[VMEM, VMEM, ANY], out_specs=[ANY], alias={2: 0},
    )
    return out


def solution(mesh):
    in_specs = (P("tm", "rows", "roll", None), P(), P(), P(), P(), P(), P())
    out_specs = P("tm", "rows", "roll", None)
    return jax.shard_map(local, mesh=mesh, in_specs=in_specs, out_specs=out_specs, check_vma=False)
```

```python
import jax
import jax.numpy as jnp
from jax import lax
from jax.experimental import pallas as pl
from jax.experimental.pallas import tpu as pltpu
from jax.sharding import PartitionSpec as P

BF = jnp.bfloat16
F32 = jnp.float32
C = 192
W = 160
S = 16
J = W // S
E = W + 2 * S
D = 240
MB = 2**20


def spread(rows, shift):
    n = lax.broadcasted_iota(jnp.int32, (rows, W), 0)
    c = lax.broadcasted_iota(jnp.int32, (rows, W), 1)
    return jnp.where((n & (S - 1)) * J + (n >> 4) - shift == c, 1.0, 0.0).astype(BF)


def gather():
    c = lax.broadcasted_iota(jnp.int32, (W, W), 0)
    n = lax.broadcasted_iota(jnp.int32, (W, W), 1)
    return jnp.where((n & (S - 1)) * J + (n >> 4) == c, 1.0, 0.0).astype(BF)


def flip(n, par):
    return n + par * (3 - 2 * n)


def act(v, gain):
    power = jnp.mean(v * v, axis=-1, keepdims=True)
    h = v * lax.rsqrt(power + 1e-06) * (gain * 0.5)
    return h + h * jnp.tanh(h)


def pack(v):
    hi = v[:, 128:]
    return jnp.concatenate([v[:, :128], jnp.concatenate([hi[:80], hi[80:]], axis=1)], axis=0)


def unpack(d):
    hi = d[W:]
    return jnp.concatenate([d[:W], jnp.concatenate([hi[:, :64], hi[:, 64:]], axis=0)], axis=1)


def edged(v):
    spot = lax.broadcasted_iota(jnp.int32, (S, C), 0)
    last = pltpu.roll(v[W - S :].astype(F32), 1, 0)
    head = pltpu.roll(v[:S].astype(F32), S - 1, 0)
    last = jnp.where(spot == 0, 0.0, last).astype(BF)
    head = jnp.where(spot == S - 1, 0.0, head).astype(BF)
    return jnp.concatenate([last, v, head], axis=0)


def place(ref, t, v, full, above=True):
    hi = full[:, 128:]
    ref[t, v, 0] = full[:, :128]
    on = jnp.concatenate([hi[S:], jnp.zeros((S, C - 128), BF)], axis=0)
    ref[t, v, 1] = jnp.concatenate([hi, on], axis=1)
    ref[t, v, 2, :, 0:64] = hi
    if above:
        ref[t, v - 1, 2, :, 64:128] = hi


def put(ref, at, v, above=True):
    place(ref, at[0], at[1], edged(v), above)


def taps(src, todo, w, par):
    ins, wts = [], []
    for t, v, a, ps in todo:
        at = {p: p + par * (2 - 2 * p) for p in ps}
        for p in ps:
            for q in range(3):
                ins.append(src[t, v + p, 0, S * q : S * q + W, :])
                wts.append(w[a, at[p], q, 0:128, :])
            ins.append(src[t, v + p, 1, 0:W, :])
            wts.append(jnp.concatenate([w[a, at[p], q, 128:C, :] for q in range(2)], axis=0))
        ps = list(ps)
        while ps:
            p = ps.pop(0)
            if ps:
                more = w[a, at[ps.pop(0)], 2, 128:C, :]
                ins.append(src[t, v + p, 2, 2 * S : E, :])
            else:
                more = jnp.zeros((C - 128, C), BF)
                ins.append(src[t, v + p, 1, 2 * S : E, :])
            wts.append(jnp.concatenate([w[a, at[p], 2, 128:C, :], more], axis=0))
    acc = jnp.zeros((W, C), F32)
    for i in range(0, len(ins), 2):
        left = jnp.concatenate(ins[i : i + 2], axis=1)
        right = jnp.concatenate(wts[i : i + 2], axis=0)
        acc = acc + jnp.dot(left, right, preferred_element_type=F32)
    return acc


def here():
    r = lax.axis_index("rows")
    keep = jnp.where((r == 0) | (r == lax.axis_size("rows") - 1), 0.0, 1.0).astype(F32)
    return r % 2, keep


def has_next():
    return lax.axis_index("tm") < lax.axis_size("tm") - 1


def has_last():
    return lax.axis_index("tm") > 0


def prep_kernel(x_ref, k_ref, own_ref, b_ref, a_ref, t_ref, d_ref):
    par, _ = here()
    m = spread(E, 1)
    g = k_ref[0:1, :]
    for t in range(4):
        for u in range(4):
            xp = jnp.dot(m, x_ref[t, flip(u, par)], preferred_element_type=F32)
            f = act(xp, g).astype(BF)
            own_ref[t, u] = f
            d = pack(f[S : S + W])
            if u < 2:
                b_ref[t, u] = d
                if t >= 2:
                    d_ref[t - 2, u] = d
            else:
                a_ref[t, 3 - u] = d
            if t >= 2:
                t_ref[t - 2, u] = d


def early_kernel(own_ref, a_ref, w1_ref, w2_ref, k_ref, r_ref, o_ref, i_ref, pe_ref, pf_ref, x_ref, s_ref):
    par, _ = here()
    for t in range(4):
        for u in range(4):
            place(x_ref, t, u, own_ref[t, u], above=u > 0)
        for k in range(2):
            put(x_ref, (t, 4 + k), unpack(a_ref[t, k]))
    bias, g = k_ref[1:2, :], k_ref[2:3, :]
    all3 = (0, 1, 2)

    def row(k, _):
        for tau in range(2):
            acc = taps(x_ref, [(tau + a, k, a, all3) for a in range(3)], w1_ref, par)
            f = act(acc + bias, g).astype(BF)
            r_ref[tau, k] = f
            put(s_ref, (tau, k + 1), f)
        o_ref[0, k] = taps(x_ref, [(0, k, 2, all3)], w1_ref, par)
        o_ref[1, k] = taps(x_ref, [(a - 1, k, a, all3) for a in (1, 2)], w1_ref, par)
        return 0

    for k in range(4):
        row(k, 0)
    for tau in range(4):
        ok = [a for a in range(3) if tau + a >= 2]
        i_ref[tau, 0] = taps(x_ref, [(tau + a - 2, -2, a, (2,)) for a in ok], w1_ref, par)
        i_ref[tau, 1] = taps(x_ref, [(tau + a - 2, -1, a, (1, 2)) for a in ok], w1_ref, par)

    @pl.when(has_next())
    def _():
        for tau in range(2):
            ok = range(2 - tau)
            pf_ref[tau, 0] = taps(s_ref, [(tau + a, -1, a, (2,)) for a in ok], w2_ref, par)
            pf_ref[tau, 1] = taps(s_ref, [(tau + a, 0, a, (1, 2)) for a in ok], w2_ref, par)
            for u in range(2):
                acc = taps(s_ref, [(tau + a, u + 1, a, all3) for a in ok], w2_ref, par)
                pe_ref[tau, u] = pack(acc.astype(BF))


def mid_kernel(bx_ref, i_ref, pe_ref, pf_ref, w1_ref, w2_ref, k_ref, r_ref, p_ref, x_ref, s_ref):
    par, keep = here()
    for t in range(4):
        for k in (1, 0):
            put(x_ref, (t, 1 - k), unpack(bx_ref[t, k]), above=k == 0)
    bias, g = k_ref[1:2, :], k_ref[2:3, :]
    for tau in range(2):
        acc = taps(x_ref, [(tau + a, 0, a, (0, 1)) for a in range(3)], w1_ref, par)
        r_ref[tau, 0] = (act(acc + i_ref[tau + 2, 0] + bias, g) * keep).astype(BF)
        acc = taps(x_ref, [(tau + a, 1, a, (0,)) for a in range(3)], w1_ref, par)
        r_ref[tau, 1] = act(acc + i_ref[tau + 2, 1] + bias, g).astype(BF)

    @pl.when(has_next())
    def _():
        for tau in range(2):
            for v in range(2):
                put(s_ref, (tau, v), r_ref[tau, v], above=v > 0)
        for tau in range(2):
            for u in range(2):
                p_ref[tau, u + 2] = pe_ref[tau, u]
            ok = range(2 - tau)
            acc = taps(s_ref, [(tau + a, 0, a, (0, 1)) for a in ok], w2_ref, par)
            p_ref[tau, 0] = pack((acc + pf_ref[tau, 0]).astype(BF))
            acc = taps(s_ref, [(tau + a, 1, a, (0,)) for a in ok], w2_ref, par)
            p_ref[tau, 1] = pack((acc + pf_ref[tau, 1]).astype(BF))


def wait_kernel(bx_ref, i_ref, re_ref, rm_ref, w1_ref, w2_ref, k_ref, in_ref, j_ref, z_ref, x_ref, s_ref):
    par, _ = here()
    for t in range(2):
        for k in (1, 0):
            put(x_ref, (t, 1 - k), unpack(bx_ref[t, k]), above=k == 0)
        for v in range(6):
            put(s_ref, (t, v), rm_ref[t, v] if v < 2 else re_ref[t, v - 2], above=v > 0)
    for tau in range(2):
        ok = [a for a in range(3) if tau + a >= 2]
        acc = taps(x_ref, [(tau + a - 2, 0, a, (0, 1)) for a in ok], w1_ref, par)
        j_ref[tau, 0] = acc + i_ref[tau, 0]
        acc = taps(x_ref, [(tau + a - 2, 1, a, (0,)) for a in ok], w1_ref, par)
        j_ref[tau, 1] = acc + i_ref[tau, 1]
    bias2 = k_ref[3:4, :]
    m = spread(W, 0)

    def row(u, _):
        at = flip(u, par)
        for tau in range(4):
            start = jnp.dot(m, in_ref[tau, at], preferred_element_type=F32) + bias2
            if tau >= 2:
                todo = [(f, u, f - tau + 4, (0, 1, 2)) for f in range(tau - 1)]
                start = start + taps(s_ref, todo, w2_ref, par)
            z_ref[tau, u] = start
        return 0

    for k in range(4):
        row(k, 0)


def recent(x_ref, r_ref, o_ref, k_ref, w1_ref, par, rows, off, fetch, scale, also):
    bias, g = k_ref[1:2, :], k_ref[2:3, :]

    @pl.when(has_last())
    def _():
        for v in (rows[0] - off, rows[0] - off + 1):
            fetch(v)
        for v in rows:
            fetch(v - off + 2)
            also(v)
            for tau in range(2):
                acc = taps(x_ref, [(tau + a, v - off, a, (0, 1, 2)) for a in range(2 - tau)], w1_ref, par)
                r_ref[tau, v - off] = scale(v, act(acc + o_ref(tau, v) + bias, g)).astype(BF)

    @pl.when(jnp.logical_not(has_last()))
    def _():
        for v in rows:
            also(v)
            for tau in range(2):
                r_ref[tau, v - off] = scale(v, act(o_ref(tau, v) + bias, g)).astype(BF)


def late_kernel(t_ref, d_ref, o_ref, j_ref, w1_ref, k_ref, r_ref, x_ref):
    par, keep = here()

    def fetch(v):
        for t in range(2):
            put(x_ref, (t, v), unpack(d_ref[t, 1 - v] if v < 2 else t_ref[t, v - 2]), above=v > 0)

    recent(
        x_ref, r_ref, lambda tau, v: j_ref[tau, v] if v < 2 else o_ref[tau, v - 2], k_ref, w1_ref, par,
        range(4), 0, fetch, lambda v, f: f if v else f * keep, lambda v: None,
    )


def last_kernel(
    t_ref, c_ref, o_ref, r_ref, z_ref, w1_ref, w2_ref, k_ref,
    out_ref, acc_ref, x_ref, s_ref, q_ref, y_ref, n_ref, sem,
):
    par, _ = here()

    def fetch(v):
        for t in range(2):
            put(x_ref, (t, v), unpack(t_ref[t, v + 2] if v < 2 else c_ref[t, v - 2]), above=v > 0)

    def ready(v):
        for n in (2 * v - 8, 2 * v - 7):
            for tau in range(2):
                put(s_ref, (tau, n), r_ref[tau, n], above=n > 0)

    recent(
        x_ref, q_ref, lambda tau, v: o_ref[tau, v - 2], k_ref, w1_ref, par,
        range(4, 6), 4, fetch, lambda v, f: f, ready,
    )
    for tau in range(2):
        for v in (4, 5):
            put(s_ref, (tau, v), q_ref[tau, v - 4])
    back = gather()

    def leave(tau, u):
        return pltpu.make_async_copy(n_ref.at[tau, u], out_ref.at[tau + 2, flip(u, par)], sem.at[tau, u])

    def finish(u):
        for tau in range(2):
            n_ref[tau, u] = jnp.dot(back, y_ref[tau, u], preferred_element_type=F32).astype(BF)
            leave(tau, u).start()

    for u in range(4):
        for tau in (2, 3, 0, 1):
            frames = [f for f in range(2) if 0 <= f - tau + 2 <= 2]
            acc = taps(s_ref, [(f, u, f - tau + 2, (0, 1, 2)) for f in frames], w2_ref, par) + z_ref[tau, u]
            if tau < 2:
                acc_ref[tau, u] = acc
            else:
                y_ref[tau - 2, u] = acc.astype(BF)
        finish(u)
    for u in range(4):
        for tau in range(2):
            leave(tau, u).wait()


def add_kernel(acc_ref, p_ref, full_ref, out_ref, n_ref, sem):
    par, _ = here()
    back = gather()
    sent = []
    for t in range(2):
        for u in range(4):
            y = (acc_ref[t, u] + unpack(p_ref[t, u]).astype(F32)).astype(BF)
            n_ref[t, u] = jnp.dot(back, y, preferred_element_type=F32).astype(BF)
            copy = pltpu.make_async_copy(n_ref.at[t, u], out_ref.at[t, flip(u, par)], sem.at[t, u])
            copy.start()
            sent.append(copy)
    for copy in sent:
        copy.wait()


VMEM = pl.BlockSpec(memory_space=pltpu.VMEM)
ANY = pl.BlockSpec(memory_space=pl.ANY)


def call(kernel, name, ins, outs, scratch, units, limit=32, in_specs=None, out_specs=None, alias={}):
    return pl.pallas_call(
        kernel,
        in_specs=in_specs or [VMEM] * len(ins),
        out_specs=out_specs or [VMEM] * len(outs),
        out_shape=[jax.ShapeDtypeStruct(s, d) for s, d in outs],
        scratch_shapes=scratch,
        compiler_params=pltpu.CompilerParams(vmem_limit_bytes=limit * MB),
        cost_estimate=pl.CostEstimate(
            flops=int(units * 6e8), bytes_accessed=3_000_000, transcendentals=500_000
        ),
        input_output_aliases=alias,
        name=name,
    )(*ins)


def local(frames_in, gain_one, conv_one, bias_one, gain_two, conv_two, bias_two):
    n = lax.axis_size("rows")
    near = [(i, i ^ 1) for i in range(n)]
    far = [(i, i + 1) for i in range(1, n - 1, 2)] + [(i + 1, i) for i in range(1, n - 1, 2)]
    diag = [(i, n + j) for i, j in far]
    kv = jnp.stack([gain_one, bias_one, gain_two, bias_two])

    own, bs, as_, ts, ds = call(
        prep_kernel, "prep", [frames_in, kv],
        [((4, 4, E, C), BF), ((4, 2, D, 128), BF), ((4, 2, D, 128), BF), ((2, 4, D, 128), BF), ((2, 2, D, 128), BF)],
        [], 40,
    )
    ar = lax.ppermute(as_, "rows", near)
    br = lax.ppermute(bs, "rows", far)
    ts, ar = lax.optimization_barrier((ts, ar))
    tr = lax.ppermute(ts, "tm", [(0, 1)])
    se, oacc, iacc, pe, pf = call(
        early_kernel, "early", [own, ar, conv_one, conv_two, kv],
        [((2, 4, W, C), BF), ((2, 4, W, C), F32), ((4, 2, W, C), F32), ((2, 2, D, 128), BF), ((2, 2, W, C), F32)],
        [pltpu.VMEM((4, 6, 3, E, 128), BF), pltpu.VMEM((2, 5, 3, E, 128), BF)], 18,
    )
    kv, ar = lax.optimization_barrier((kv + 0.0 * ar[0, 0, 0, 0].astype(F32), ar))
    ds, kv = lax.optimization_barrier((ds, kv))
    dr = lax.ppermute(ds, ("tm", "rows"), diag)
    sm, ps = call(
        mid_kernel, "mid", [br, iacc, pe, pf, conv_one, conv_two, kv],
        [((2, 2, W, C), BF), ((2, 4, D, 128), BF)],
        [pltpu.VMEM((4, 2, 3, E, 128), BF), pltpu.VMEM((2, 2, 3, E, 128), BF)], 3,
    )
    pr = lax.ppermute(ps, "tm", [(0, 1)])
    jacc, zacc = call(
        wait_kernel, "wait", [br, iacc, se, sm, conv_one, conv_two, kv, frames_in],
        [((2, 2, W, C), F32), ((4, 4, W, C), F32)],
        [pltpu.VMEM((2, 2, 3, E, 128), BF), pltpu.VMEM((2, 6, 3, E, 128), BF)], 20,
    )
    tr, zacc = lax.optimization_barrier((tr, zacc))
    cr = lax.ppermute(jnp.stack([tr[:, 3], tr[:, 2]], axis=1), "rows", near)
    (rs,) = call(
        late_kernel, "late", [tr, dr, oacc, jacc, conv_one, kv], [((2, 4, W, C), BF)],
        [pltpu.VMEM((2, 6, 3, E, 128), BF)], 1,
    )
    rs, cr = lax.optimization_barrier((rs, cr))
    out, acc = call(
        last_kernel, "last", [tr, cr, oacc, rs, zacc, conv_one, conv_two, kv],
        [((4, 4, W, C), BF), ((2, 4, W, C), F32)],
        [
            pltpu.VMEM((2, 4, 3, E, 128), BF), pltpu.VMEM((2, 6, 3, E, 128), BF), pltpu.VMEM((2, 2, W, C), BF),
            pltpu.VMEM((2, 4, W, C), BF), pltpu.VMEM((2, 4, W, C), BF), pltpu.SemaphoreType.DMA((2, 4)),
        ],
        1, out_specs=[ANY, VMEM],
    )
    (out,) = call(
        add_kernel, "add", [acc, pr, out], [((4, 4, W, C), BF)],
        [pltpu.VMEM((2, 4, W, C), BF), pltpu.SemaphoreType.DMA((2, 4))],
        1, in_specs=[VMEM, VMEM, ANY], out_specs=[ANY], alias={2: 0},
    )
    return out


def solution(mesh):
    in_specs = (P("tm", "rows", "roll", None), P(), P(), P(), P(), P(), P())
    out_specs = P("tm", "rows", "roll", None)
    return jax.shard_map(local, mesh=mesh, in_specs=in_specs, out_specs=out_specs, check_vma=False)
```
